32 devices in a mesh: space: 8 (over z, x), tile: 4 (over y, core).
Axes of the slice: x: 2, y: 2, z: 4, core: 2. Of those that a mesh axis runs over, the one named last changes fastest.
Arguments:
- eigenvectors: float32 [2, 256, 3, 32768], P(None, None, None, ('space', 'tile')), may hold values from -6 to 6
- perambulator: float32 [2, 1024, 1024], P(None, 'space'), may hold values from -6 to 6
- momenta: int32 [2, 3], replicated, may hold values from 1 to 2
- graph_blocks: int32 [32, 2], replicated, may hold values from 0 to 7
Outputs:
- elementals: float32 [2, 2, 256, 256], P(None, None, 'tile', 'space')
- contractions: float32 [32, 2, 256, 256], P(('space', 'tile'))
The draws below stay inside these ranges and needn't reach their ends.
All inputs are finite; a program needn't handle non-finite values.
Results may differ from the reference program's by a relative error of at most 0.00016.
Values sent between devices are 32-bit elements; how exact they have to be, the bound alone decides.
No kernel may reach another device: no remote copies, remote signals or barrier semaphores. Data moves between devices by JAX's collectives and lax.ppermute only.
A program may use at most 64 MiB of HBM per device.

```python
import math
import jax
import jax.numpy as jnp
import numpy as np
from jax import lax

NEV = 256
NC = 3
NMOM = 2
SITES_DEV = 1024
SITES = 32768
ORDER = 1024
BLOCK = 256
NBLK = 8
NGRAPH = 32
N_TILE = 4
DEVICES = 32


def set_ends(array, key, low, high):
    dims = array.shape
    place = [jax.random.randint(jax.random.fold_in(key, axis), (), 0, dims[axis]) for axis in range(len(dims))]
    array = array.at[tuple(place)].set(low)
    longest = dims.index(max(dims))
    place[longest] = (place[longest] + 1) % dims[longest]
    return array.at[tuple(place)].set(high)


def block_scale(key, shape, pieces, smallest, high):
    gain = 1.0
    for dim, shards_of in pieces:
        steps = jax.random.uniform(jax.random.fold_in(jax.random.fold_in(key, 6), dim), (shards_of,), jnp.float32, smallest / len(pieces), high / len(pieces))
        gain = gain * jnp.repeat(jnp.exp(steps), shape[dim] // shards_of).reshape((-1,) + (1,) * (len(shape) - 1 - dim))
    return gain


def rank_table(amount, lean):
    loads = [(1 << 20) // math.isqrt(standing ** lean) + 1 for standing in range(1, amount + 1)]
    scale = 1 + sum(loads) // (1 << 30)
    return np.cumsum(np.array([max(1, weight // scale) for weight in loads]))


def ranked(own_key, dims, count, skew):
    listing = rank_table(count, skew)
    pick = jax.random.randint(jax.random.fold_in(own_key, 1), dims, 0, int(listing[count - 1]))
    grade = jnp.searchsorted(jnp.asarray(listing, jnp.int32), pick, side="right")
    return jax.random.permutation(jax.random.fold_in(own_key, 2), count)[grade].astype(jnp.int32)


def bell_draw(stream_key, extent, deviation, bound, pieces=(), kind=jnp.bfloat16):
    values = deviation * jax.random.normal(stream_key, extent, jnp.float32)
    if pieces:
        values = values * block_scale(stream_key, extent, pieces, -0.22, 0.18)
    return jnp.clip(values, -bound, bound).astype(kind)


def setup_inputs(seed: int = 0) -> dict:
    key_list = jax.random.split(jax.random.key(seed), 5)
    return {
        "eigenvectors": bell_draw(key_list[0], (2, NEV, NC, SITES), 1.0, 6.0, ((3, 32),), jnp.float32),
        "perambulator": bell_draw(key_list[1], (2, ORDER, ORDER), 1.0, 6.0, ((1, 8),), jnp.float32),
        "momenta": set_ends(jax.random.randint(key_list[2], (NMOM, 3), 1, 3), jax.random.fold_in(key_list[2], 1), 1, 2).astype(jnp.int32),
        "graph_blocks": set_ends(ranked(key_list[3], (NGRAPH, 2), NBLK, 2), jax.random.fold_in(key_list[3], 3), 0, NBLK - 1).astype(jnp.int32),
    }


lattice_edge = 64

def inner_product(left, right):
    return lax.dot_general(left, right, (((1,), (1,)), ((), ())), precision=lax.Precision.HIGHEST, preferred_element_type=jnp.float32)

def phased_gram(vectors, momenta, first_site):
    vector_count = vectors.shape[1]
    site_index = first_site + lax.iota(jnp.int32, vectors.shape[3])
    x_pos = site_index % lattice_edge
    y_pos = site_index // lattice_edge % lattice_edge
    z_pos = site_index // (lattice_edge * lattice_edge)
    wave_number = (momenta[:, 0:1] * x_pos[None, :] + momenta[:, 1:2] * y_pos[None, :] + momenta[:, 2:3] * z_pos[None, :]) % lattice_edge
    phase_angle = wave_number.astype(jnp.float32) * (2.0 * math.pi / lattice_edge)
    cosine = jnp.cos(phase_angle)
    sine_part = jnp.sin(phase_angle)
    real_part = vectors[0]
    imag_part = vectors[1]
    flat_real = real_part.reshape(vector_count, -1)
    flat_imag = imag_part.reshape(vector_count, -1)
    stacked = []
    for moment in range(momenta.shape[0]):
        cos_row = cosine[moment][None, None, :]
        sin_row = sine_part[moment][None, None, :]
        phased_real = (cos_row * real_part + sin_row * imag_part).reshape(vector_count, -1)
        phased_imag = (cos_row * imag_part - sin_row * real_part).reshape(vector_count, -1)
        gram_real = inner_product(flat_real, phased_real) + inner_product(flat_imag, phased_imag)
        gram_imag = inner_product(flat_real, phased_imag) - inner_product(flat_imag, phased_real)
        stacked.append(jnp.stack([gram_real, gram_imag]))
    return jnp.stack(stacked)

def transport(elementals_rows, perambulator_part):
    sources = perambulator_part.shape[1]
    vector_count = elementals_rows.shape[3]
    tensor = perambulator_part.reshape(2, sources, vector_count, -1)

    def apply_part(tau_part, phi_part):
        return jnp.einsum('cja,mij->mcia', tau_part, phi_part, precision=lax.Precision.HIGHEST, preferred_element_type=jnp.float32)
    mixed_real = apply_part(tensor[0], elementals_rows[:, 0]) - apply_part(tensor[1], elementals_rows[:, 1])
    mixed_imag = apply_part(tensor[0], elementals_rows[:, 1]) + apply_part(tensor[1], elementals_rows[:, 0])
    row_total = elementals_rows.shape[2] * tensor.shape[3]
    result = jnp.stack([mixed_real, mixed_imag], axis=1)
    return result.reshape(result.shape[0], 2, sources, row_total) * (1.0 / math.sqrt(vector_count))

def pair_product(left, right):

    def contract(first, second):
        return jnp.einsum('gcr,gcs->grs', first, second, precision=lax.Precision.HIGHEST, preferred_element_type=jnp.float32)
    pair_real = contract(left[:, 0], right[:, 0]) - contract(left[:, 1], right[:, 1])
    pair_imag = contract(left[:, 0], right[:, 1]) + contract(left[:, 1], right[:, 0])
    return jnp.stack([pair_real, pair_imag], axis=1)

def reference(eigenvectors, perambulator, momenta, graph_blocks):

    def accumulate(block_index, total):
        first_site = block_index.astype(jnp.int32) * SITES_DEV
        piece = lax.dynamic_slice_in_dim(eigenvectors, first_site, SITES_DEV, 3)
        return total + phased_gram(piece, momenta, first_site)
    gram = lax.fori_loop(0, DEVICES, accumulate, jnp.zeros((NMOM, 2, NEV, NEV), jnp.float32))
    elementals = gram * (1.0 / math.sqrt(NC * SITES))
    mixed_rows = transport(elementals, perambulator)
    blocks = mixed_rows.reshape(NMOM, 2, ORDER, N_TILE, BLOCK).transpose(0, 3, 1, 2, 4).reshape(NBLK, 2, ORDER, BLOCK)

    def one_graph(pair_ids):
        left = lax.dynamic_index_in_dim(blocks, pair_ids[0], 0, keepdims=True)
        right = lax.dynamic_index_in_dim(blocks, pair_ids[1], 0, keepdims=True)
        return pair_product(left, right)[0]
    contractions = lax.map(one_graph, graph_blocks) * (1.0 / math.sqrt(ORDER))
    return (elementals, contractions)
```

```python
import functools
import math

import jax
import jax.numpy as jnp
from jax import lax
from jax.experimental import pallas as pl
from jax.experimental.pallas import tpu as pltpu
from jax.sharding import PartitionSpec as P

LATTICE_EDGE = 64
LANES = 128
F32 = jnp.float32
BF16 = jnp.bfloat16
VMEM_LIMIT = 48 * 1024 * 1024


def bits_of(count):
    return range(count.bit_length() - 1)


def split(value):
    high = value.astype(BF16)
    return high, (value - high.astype(F32)).astype(BF16)


def dot_nt(left, right):
    return lax.dot_general(left, right, (((1,), (1,)), ((), ())), preferred_element_type=F32)


def dot_tn(left, right):
    return lax.dot_general(left, right, (((0,), (0,)), ((), ())), preferred_element_type=F32)


def gram_kernel(momenta, first_site, vectors, total, *, chunks, norm):
    step = pl.program_id(0)
    width = vectors.shape[3]

    @pl.when(step == 0)
    def _():
        total[...] = jnp.zeros_like(total)

    site = first_site[0] + (step % chunks) * width + lax.broadcasted_iota(jnp.int32, (1, width), 1)
    x_pos = site % LATTICE_EDGE
    y_pos = site // LATTICE_EDGE % LATTICE_EDGE
    z_pos = site // (LATTICE_EDGE * LATTICE_EDGE)
    real = vectors[0, 0]
    imag = vectors[1, 0]
    real_hi, real_lo = split(real)
    imag_hi, imag_lo = split(imag)
    left_hi = jnp.concatenate([real_hi, imag_hi], axis=0)
    left_lo = jnp.concatenate([real_lo, imag_lo], axis=0)
    count = real.shape[0]

    def product(right):
        hi, lo = split(right)
        return dot_nt(left_hi, hi) + dot_nt(left_hi, lo) + dot_nt(left_lo, hi)

    for p in range(total.shape[0]):
        wave = (momenta[p, 0] * x_pos + momenta[p, 1] * y_pos + momenta[p, 2] * z_pos) % LATTICE_EDGE
        theta = wave.astype(F32) * (2.0 * math.pi / LATTICE_EDGE)
        cosine, sine = jnp.cos(theta), jnp.sin(theta)
        by_real = product(cosine * real + sine * imag)
        by_imag = product(cosine * imag - sine * real)
        total[p, 0] += by_real[:count] + by_imag[count:]
        total[p, 1] += by_imag[:count] - by_real[count:]

    @pl.when(step == pl.num_programs(0) - 1)
    def _():
        total[...] *= norm


def local_gram(vectors, momenta, first_site, norm):
    planes = vectors.transpose(0, 2, 1, 3)
    _, colours, count, sites = planes.shape
    width = min(sites, 512)
    chunks = sites // width
    moments = momenta.shape[0]
    return pl.pallas_call(
        functools.partial(gram_kernel, chunks=chunks, norm=norm),
        grid=(colours * chunks,),
        in_specs=[
            pl.BlockSpec(memory_space=pltpu.SMEM),
            pl.BlockSpec(memory_space=pltpu.SMEM),
            pl.BlockSpec((2, 1, count, width), lambda s: (0, s // chunks, 0, s % chunks)),
        ],
        out_specs=pl.BlockSpec((moments, 2, count, count), lambda s: (0, 0, 0, 0)),
        out_shape=jax.ShapeDtypeStruct((moments, 2, count, count), F32),
        compiler_params=pltpu.CompilerParams(vmem_limit_bytes=VMEM_LIMIT),
        cost_estimate=pl.CostEstimate(
            flops=24 * moments * count * count * colours * sites,
            bytes_accessed=8 * count * colours * sites,
            transcendentals=0,
        ),
        name="local_gram",
    )(momenta, first_site, planes)


def swap(value, axis, bit):
    size = lax.axis_size(axis)
    return lax.ppermute(value, axis, [(i, i ^ (1 << bit)) for i in range(size)])


def shift(value, axis, by):
    size = lax.axis_size(axis)
    return lax.ppermute(value, axis, [(i, i + by) for i in range(size) if 0 <= i + by < size])


def own_bit(axis, bit):
    return (lax.axis_index(axis) >> bit) & 1


def halve(value, axis, bit):
    mine = own_bit(axis, bit)
    half = value.shape[0] // 2
    away = lax.dynamic_slice_in_dim(value, (1 - mine) * half, half, 0)
    kept = lax.dynamic_slice_in_dim(value, mine * half, half, 0)
    return kept + swap(away, axis, bit)


def double(value, axis, bit):
    other = swap(value, axis, bit)
    return jnp.where(
        own_bit(axis, bit) == 0,
        jnp.concatenate([value, other]),
        jnp.concatenate([other, value]),
    )


def sum_everywhere(rows):
    tile_bits = [("tile", b) for b in bits_of(lax.axis_size("tile"))]
    space_bits = [("space", b) for b in bits_of(lax.axis_size("space"))]
    scattered = tile_bits + space_bits[:1]
    for axis, bit in scattered:
        rows = halve(rows, axis, bit)
    for axis, bit in space_bits[1:]:
        rows = rows + swap(rows, axis, bit)
    for axis, bit in scattered[::-1]:
        rows = double(rows, axis, bit)
    return rows


def gather_perambulator(part):
    half = part.shape[1] // 2
    part = lax.dynamic_slice_in_dim(part, own_bit("tile", 0) * half, half, 1)
    spin = 4
    own = part.reshape(2, half, -1, spin).transpose(0, 3, 1, 2)
    length = lax.axis_size("space") // 2
    place = lax.axis_index("space") // 2
    below, above = [own], [own]
    for _ in range(length - 1):
        below.append(shift(below[-1], "space", 2))
        above.append(shift(above[-1], "space", -2))
    column = [own]
    for s in range(1, length):
        column.append(jnp.where(place >= s, below[s], above[length - s]))
    plane = column + [swap(piece, "space", 0) for piece in column]
    return plane + [swap(piece, "tile", 0) for piece in plane]


def pair_kernel(blocks, elementals, order, *refs, pieces, scale):
    sources = refs[:pieces]
    out = refs[pieces]
    tau, left_hi, left_lo, right_hi, right_lo, woven, arrived = refs[pieces + 1 :]
    for n in range(pieces):
        pltpu.make_async_copy(sources[n], tau.at[n], arrived.at[n]).start()
    _, spin, depth, count = tau.shape[1:]
    rows = left_hi.shape[1] // (2 * spin)
    tiles = count // rows
    real_rows, imag_rows = [], []
    for side in range(2):
        block = blocks[side]
        p = block // tiles
        first = pl.multiple_of(block % tiles * rows, rows)
        real = elementals[p, 0, pl.ds(first, rows), :]
        imag = elementals[p, 1, pl.ds(first, rows), :]
        real_rows += [real, imag]
        imag_rows += [-imag, real]
    weights = jnp.concatenate(
        [jnp.concatenate(real_rows, axis=0), jnp.concatenate(imag_rows, axis=0)], axis=1
    )
    weights_hi, weights_lo = split(weights)
    for n in range(pieces):
        pltpu.make_async_copy(sources[n], tau.at[n], arrived.at[n]).wait()
        given = jnp.concatenate(
            [tau[n, 0].reshape(spin * depth, count), tau[n, 1].reshape(spin * depth, count)], axis=1
        )
        given_hi, given_lo = split(given)
        mixed = dot_nt(given_hi, weights_hi) + dot_nt(given_hi, weights_lo) + dot_nt(given_lo, weights_hi)
        mixed_hi, mixed_lo = split(mixed)
        here = pl.ds(n * depth, depth)
        for a in range(spin):
            lanes = pl.ds(a * 2 * rows, 2 * rows)
            left_hi[here, lanes] = mixed_hi[a * depth : (a + 1) * depth, : 2 * rows]
            left_lo[here, lanes] = mixed_lo[a * depth : (a + 1) * depth, : 2 * rows]
            right_hi[here, lanes] = mixed_hi[a * depth : (a + 1) * depth, 2 * rows :]
            right_lo[here, lanes] = mixed_lo[a * depth : (a + 1) * depth, 2 * rows :]
    pair = (
        dot_tn(left_hi[...], right_hi[...])
        + dot_tn(left_hi[...], right_lo[...])
        + dot_tn(left_lo[...], right_hi[...])
    ) * scale
    pair_hi, pair_lo = split(pair)
    placed = jnp.dot(pair_hi, order[...], preferred_element_type=F32) + jnp.dot(
        pair_lo, order[...], preferred_element_type=F32
    )
    width = rows * spin
    for a in range(spin):
        top = placed[2 * a * rows : (2 * a + 1) * rows]
        low = placed[(2 * a + 1) * rows : (2 * a + 2) * rows]
        parts = top[:, :width] - low[:, width:], top[:, width:] + low[:, :width]
        for n, value in enumerate(parts):
            for c in range(width // LANES):
                woven[n, c, pl.ds(a, rows, stride=spin), :] = value[:, c * LANES : (c + 1) * LANES]
    for n in range(2):
        for c in range(width // LANES):
            out[n, :, c * LANES : (c + 1) * LANES] = woven[n, c]


def lane_order(rows, spin):
    size = 2 * rows * spin
    lane = lax.iota(jnp.int32, size)
    a, part, i = lane // (2 * rows), lane // rows % 2, lane % rows
    target = part * rows * spin + i * spin + a
    return (target[:, None] == lane[None, :]).astype(BF16)


def pair_contraction(blocks, elementals, pieces, scale):
    _, spin, depth, count = pieces[0].shape
    rows = count // lax.axis_size("tile")
    size = 2 * rows * spin
    number = len(pieces)
    stored = pltpu.VMEM((number * depth, size), BF16)
    return pl.pallas_call(
        functools.partial(pair_kernel, pieces=number, scale=scale),
        in_specs=[
            pl.BlockSpec(memory_space=pltpu.SMEM),
            pl.BlockSpec(memory_space=pltpu.VMEM),
            pl.BlockSpec(memory_space=pltpu.VMEM),
        ]
        + [pl.BlockSpec(memory_space=pl.ANY)] * number,
        out_specs=pl.BlockSpec(memory_space=pltpu.VMEM),
        out_shape=jax.ShapeDtypeStruct((2, rows * spin, rows * spin), F32),
        scratch_shapes=[
            pltpu.VMEM((number,) + pieces[0].shape, F32),
            stored,
            stored,
            stored,
            stored,
            pltpu.VMEM((2, rows * spin // LANES, rows * spin, LANES), F32),
            pltpu.SemaphoreType.DMA((number,)),
        ],
        compiler_params=pltpu.CompilerParams(vmem_limit_bytes=VMEM_LIMIT),
        name="pair_contraction",
    )(blocks, elementals, lane_order(rows, spin), *pieces)


def per_device(eigenvectors, perambulator, momenta, graph_blocks):
    space_count = lax.axis_size("space")
    tile_count = lax.axis_size("tile")
    space_index = lax.axis_index("space")
    tile_index = lax.axis_index("tile")
    device = space_index * tile_count + tile_index
    _, count, colours, sites = eigenvectors.shape
    order = perambulator.shape[2]
    first_site = (device * sites).astype(jnp.int32).reshape(1)
    norm = 1.0 / math.sqrt(colours * sites * space_count * tile_count)
    pieces = gather_perambulator(perambulator)
    partial = local_gram(eigenvectors, momenta, first_site, norm)
    full = sum_everywhere(partial.reshape(-1, count)).reshape(partial.shape)
    rows, columns = count // tile_count, count // space_count
    elementals = lax.dynamic_slice(
        full, (0, 0, tile_index * rows, space_index * columns), full.shape[:2] + (rows, columns)
    )
    scale = 1.0 / (count * math.sqrt(order))
    contractions = pair_contraction(graph_blocks[device], full, pieces, scale)
    return elementals, contractions[None]


def solution(mesh):
    in_specs = (P(None, None, None, ("space", "tile")), P(None, "space", None), P(), P())
    out_specs = (P(None, None, "tile", "space"), P(("space", "tile"), None, None, None))
    return jax.shard_map(
        per_device, mesh=mesh, in_specs=in_specs, out_specs=out_specs, check_vma=False
    )
```

```python
import functools
import math

import jax
import jax.numpy as jnp
from jax import lax
from jax.experimental import pallas as pl
from jax.experimental.pallas import tpu as pltpu
from jax.sharding import PartitionSpec as P

LATTICE_EDGE = 64
LANES = 128
F32 = jnp.float32
BF16 = jnp.bfloat16
GRAM_VMEM = 56 * 1024 * 1024
PAIR_VMEM = 60 * 1024 * 1024


def bits_of(count):
    return range(count.bit_length() - 1)


def split(value):
    high = value.astype(BF16)
    return high, (value - high.astype(F32)).astype(BF16)


def dot_nt(left, right):
    return lax.dot_general(left, right, (((1,), (1,)), ((), ())), preferred_element_type=F32)


def product(left, right):
    return dot_nt(left[0], right[0]) + dot_nt(left[0], right[1]) + dot_nt(left[1], right[0])


def dot_tn(left, right):
    return lax.dot_general(left, right, (((0,), (0,)), ((), ())), preferred_element_type=F32)


def gram_kernel(momenta, vectors, *refs, width, norm):
    away, kept, held, arrived = refs[-4:]
    _, colours, _, sites = vectors.shape
    core = lax.rem(lax.axis_index("tile"), 2)
    first_site = (lax.axis_index("space") * lax.axis_size("tile") + lax.axis_index("tile")) * sites
    chunks = sites // width
    copies = []
    for colour in range(colours):
        for chunk in range(chunks):
            lanes = pl.ds(chunk * width, width)
            copies.append(
                pltpu.make_async_copy(
                    vectors.at[:, colour, :, lanes], held.at[:, colour, :, lanes], arrived.at[len(copies)]
                )
            )
    for copy in copies:
        copy.start()
    half = kept.shape[0]
    sums = []
    for total, first in ((kept, core * half), (away, (1 - core) * half)):
        for p in range(half):
            phases = []
            for chunk in range(chunks):
                site = first_site + chunk * width + lax.broadcasted_iota(jnp.int32, (1, width), 1)
                wave = (
                    momenta[first + p, 0] * (site % LATTICE_EDGE)
                    + momenta[first + p, 1] * (site // LATTICE_EDGE % LATTICE_EDGE)
                    + momenta[first + p, 2] * (site // (LATTICE_EDGE * LATTICE_EDGE))
                ) % LATTICE_EDGE
                theta = wave.astype(F32) * (2.0 * math.pi / LATTICE_EDGE)
                phases.append((jnp.cos(theta), jnp.sin(theta)))
            sums.append((total, p, phases))
    held_sums = {}
    for n, copy in enumerate(copies):
        copy.wait()
        chunk = n % chunks
        real = held[0, n // chunks, :, chunk * width : (chunk + 1) * width]
        imag = held[1, n // chunks, :, chunk * width : (chunk + 1) * width]
        left = split(real), split(imag), split(real - imag)
        for number, (_, _, phases) in enumerate(sums):
            cosine, sine = phases[chunk]
            phased_real = cosine * real + sine * imag
            phased_imag = cosine * imag - sine * real
            by_real = product(left[2], split(phased_real))
            from_real = product(left[0], split(phased_imag - phased_real))
            from_imag = product(left[1], split(phased_real + phased_imag))
            parts = by_real, from_real, from_imag
            held_sums[number] = parts if n == 0 else [old + new for old, new in zip(held_sums[number], parts)]
    for number, (total, p, _) in enumerate(sums):
        by_real, from_real, from_imag = held_sums[number]
        total[p, 0] = (by_real + from_imag) * norm
        total[p, 1] = (by_real + from_real) * norm


def local_gram(planes, momenta, norm, started):
    _, colours, count, sites = planes.shape
    half = momenta.shape[0] // 2
    width = min(sites, 512)
    return pl.pallas_call(
        functools.partial(gram_kernel, width=width, norm=norm),
        in_specs=[pl.BlockSpec(memory_space=pltpu.SMEM), pl.BlockSpec(memory_space=pltpu.HBM)]
        + [pl.BlockSpec(memory_space=pl.ANY)] * len(started),
        out_specs=[pl.BlockSpec(memory_space=pltpu.VMEM)] * 2,
        out_shape=[jax.ShapeDtypeStruct((half, 2, count, count), F32)] * 2,
        scratch_shapes=[
            pltpu.VMEM(planes.shape, F32),
            pltpu.SemaphoreType.DMA((colours * sites // width,)),
        ],
        compiler_params=pltpu.CompilerParams(vmem_limit_bytes=GRAM_VMEM),
        cost_estimate=pl.CostEstimate(
            flops=48 * half * count * count * colours * sites,
            bytes_accessed=8 * count * colours * sites,
            transcendentals=0,
        ),
        name="local_gram",
    )(momenta, planes, *started)


def after(value, others):
    if not others:
        return value
    anywhere = pl.BlockSpec(memory_space=pl.ANY)
    return pl.pallas_call(
        lambda *refs: None,
        in_specs=[anywhere] * (1 + len(others)),
        out_specs=anywhere,
        out_shape=jax.ShapeDtypeStruct(value.shape, value.dtype),
        input_output_aliases={0: 0},
        compiler_params=pltpu.CompilerParams(vmem_limit_bytes=1024 * 1024),
        name="after",
    )(value, *others)


def swap(value, axis, bit):
    size = lax.axis_size(axis)
    return lax.ppermute(value, axis, [(i, i ^ (1 << bit)) for i in range(size)])


def shift(value, axis, by):
    size = lax.axis_size(axis)
    return lax.ppermute(value, axis, [(i, i + by) for i in range(size) if 0 <= i + by < size])


def own_bit(axis, bit):
    return (lax.axis_index(axis) >> bit) & 1


def halve(value, axis, bit):
    mine = own_bit(axis, bit)
    half = value.shape[0] // 2
    away = lax.dynamic_slice_in_dim(value, (1 - mine) * half, half, 0)
    kept = lax.dynamic_slice_in_dim(value, mine * half, half, 0)
    return kept + swap(away, axis, bit)


def both(value, axis, bit):
    return value + swap(value, axis, bit)


def double(value, axis, bit):
    other = swap(value, axis, bit)
    return jnp.where(
        own_bit(axis, bit) == 0,
        jnp.concatenate([value, other]),
        jnp.concatenate([other, value]),
    )


def deal_kernel(tau, travel, rest, *, by_core, by_tile, tiles):
    parts, spin, _, count = travel.shape
    tile = lax.axis_index("tile")
    core = lax.rem(tile, 2)
    groups = [(pl.multiple_of(core * by_core, 8), by_core, travel, 0, pl.ds(0, by_core))]
    shared = 2 * by_core
    if by_tile:
        for n in range(tiles // 2):
            first = pl.multiple_of(shared + (2 * n + core) * by_tile, 8)
            groups.append((first, by_tile, rest, n * by_tile, None))
        first = pl.multiple_of(shared + tile * by_tile, 8)
        groups.append((first, by_tile, travel, by_core, None))
    rows = jnp.concatenate(
        [tau[part, pl.ds(first, depth), :] for part in range(parts) for first, depth, *_ in groups], axis=0
    )
    width = min(count, LANES)
    line = lax.broadcasted_iota(jnp.int32, (spin * width, spin * width), 0)
    lane = lax.broadcasted_iota(jnp.int32, (spin * width, spin * width), 1)
    order = (line == lane % width * spin + lane // width).astype(BF16)
    for block in range(count // width):
        value = rows[:, block * spin * width : (block + 1) * spin * width]
        high = value.astype(BF16)
        left = value - high.astype(F32)
        middle, low = split(left)
        moved = (
            jnp.dot(high, order, preferred_element_type=F32)
            + jnp.dot(middle, order, preferred_element_type=F32)
        ) + jnp.dot(low, order, preferred_element_type=F32)
        top = 0
        for part in range(parts):
            for _, depth, target, at, _ in groups:
                for a in range(spin):
                    target[part, a, at : at + depth, block * width : (block + 1) * width] = moved[
                        top : top + depth, a * width : (a + 1) * width
                    ]
                top += depth


def deal(part, spin, by_core, by_tile):
    parts, _, order = part.shape
    tiles = lax.axis_size("tile")
    shape = (parts, spin, by_core + by_tile, order // spin)
    rest = (parts, spin, max(tiles // 2 * by_tile, 8), order // spin)
    return pl.pallas_call(
        functools.partial(deal_kernel, by_core=by_core, by_tile=by_tile, tiles=tiles),
        in_specs=[pl.BlockSpec(memory_space=pltpu.VMEM)],
        out_specs=[pl.BlockSpec(memory_space=pltpu.VMEM)] * 2,
        out_shape=[jax.ShapeDtypeStruct(shape, F32), jax.ShapeDtypeStruct(rest, F32)],
        compiler_params=pltpu.CompilerParams(vmem_limit_bytes=GRAM_VMEM),
        name="deal",
    )(part)


def exchange_everything(part, gram):
    space_bits, tile_bits = bits_of(lax.axis_size("space")), bits_of(lax.axis_size("tile"))
    tile_count = lax.axis_size("tile")
    sources = part.shape[1]
    shared = sources // 4
    if (sources - shared) // tile_count % 8:
        shared = sources
    by_core, by_tile = shared // 2, (sources - shared) // tile_count
    mixed, rest = deal(part, 4, by_core, by_tile)
    pieces = [(mixed, by_core)]
    if by_tile:
        pieces.append((rest, rest.shape[2]))

    slots, rounds, spread = {0: mixed}, [], None
    for r in range(1, len(space_bits) + 2):
        arrived = []
        masks = [mask for mask in range(1, lax.axis_size("space")) if mask.bit_count() == r]
        for mask in masks:
            low = mask & -mask
            slots[mask] = swap(slots[mask ^ low], "space", low.bit_length() - 1)
            arrived.append(slots[mask])
        if spread is not None:
            for bit in tile_bits[1:]:
                arrived.append(swap(spread, "tile", bit))
                spread = jnp.concatenate([spread, arrived[-1]], axis=2)
        spread = None
        if masks and by_tile:
            spread = jnp.concatenate([slots[mask][:, :, by_core:] for mask in masks], axis=2)
        rounds.append(arrived)
        pieces += [(piece, piece.shape[2]) for piece in arrived]

    away, kept = gram([mixed])
    away = after(away.reshape(-1, kept.shape[-1]), rounds[0])
    rows = kept.reshape(-1, kept.shape[-1]) + swap(away, "tile", 0)
    steps = [(halve, "tile", b) for b in tile_bits[1:]]
    steps += [(halve, "space", b) for b in space_bits[:1]]
    steps += [(both, "space", b) for b in space_bits[1:]]
    middle = len(steps) - 2
    steps += [(double, axis, b) for step, axis, b in steps[::-1] if step is halve]
    ends = {middle: 1, middle + 2: 2, len(steps) - 1: 3}
    for n, (step, axis, bit) in enumerate(steps):
        rows = step(rows, axis, bit)
        if n in ends:
            rows = after(rows, rounds[ends[n]] if ends[n] < len(rounds) else [])
    return rows, swap(rows, "tile", 0), pieces


def pair_kernel(blocks, own, other, order, *refs, depths, scale):
    sources = refs[: len(depths)]
    away, kept, left, right, woven, tau, held, placing, arrived = refs[len(depths) :]
    _, spin, total, count = tau.shape
    outs = (away, kept)
    rows = left.shape[3] // 2
    tiles = count // rows
    half = own.shape[0]
    core = lax.rem(lax.axis_index("tile"), 2)
    gathered = [
        pltpu.make_async_copy(own, held.at[pl.ds(core * half, half)], arrived.at[len(depths)]),
        pltpu.make_async_copy(other, held.at[pl.ds((1 - core) * half, half)], arrived.at[len(depths) + 1]),
    ]
    copies, first = [], 0
    for n, depth in enumerate(depths):
        target = tau.at[:, :, pl.ds(first, depth)]
        copies.append(pltpu.make_async_copy(sources[n].at[:, :, pl.ds(0, depth)], target, arrived.at[n]))
        first += depth
    last = pltpu.make_async_copy(order, placing, arrived.at[len(depths) + 2])
    for copy in [*gathered, *copies, last]:
        copy.start()
    for copy in gathered:
        copy.wait()
    real_rows, imag_rows = [], []
    for side in range(4):
        block = blocks[side // 2, side % 2]
        p = block // tiles
        start = pl.multiple_of(block % tiles * rows, rows)
        real = held[p, 0, pl.ds(start, rows), :]
        imag = held[p, 1, pl.ds(start, rows), :]
        real_rows += [real, imag]
        imag_rows += [-imag, real]
    weights = split(
        jnp.concatenate([jnp.concatenate(real_rows, axis=0), jnp.concatenate(imag_rows, axis=0)], axis=1)
    )
    depth = min(total, 256)
    for n in range(total // depth):
        while copies and sum(depths[: len(depths) - len(copies)]) < (n + 1) * depth:
            copies.pop(0).wait()
        here = pl.ds(n * depth, depth)

        def mix(a, carry):
            given = jnp.concatenate([tau[0, a, here, :], tau[1, a, here, :]], axis=1)
            mixed = product(split(given), weights)
            for g in range(2):
                left[g, a, here, :] = mixed[:, 4 * g * rows : (4 * g + 2) * rows]
                right[g, a, here, :] = mixed[:, (4 * g + 2) * rows : (4 * g + 4) * rows]
            return carry

        lax.fori_loop(0, spin, mix, 0)
    last.wait()
    width = rows * spin
    for g, out in enumerate(outs):
        left_hi, left_lo = split(jnp.concatenate([left[g, a] for a in range(spin)], axis=1))
        right_hi, right_lo = split(jnp.concatenate([right[g, a] for a in range(spin)], axis=1))
        pair = (dot_tn(left_hi, right_hi) + dot_tn(left_hi, right_lo) + dot_tn(left_lo, right_hi)) * scale
        pair_hi, pair_lo = split(pair)
        placed = jnp.dot(pair_hi, placing[...], preferred_element_type=F32) + jnp.dot(
            pair_lo, placing[...], preferred_element_type=F32
        )
        for a in range(spin):
            top = placed[2 * a * rows : (2 * a + 1) * rows]
            low = placed[(2 * a + 1) * rows : (2 * a + 2) * rows]
            parts = top[:, :width] - low[:, width:], top[:, width:] + low[:, :width]
            for n, value in enumerate(parts):
                for c in range(width // LANES):
                    woven[n, c, pl.ds(a, rows, stride=spin), :] = value[:, c * LANES : (c + 1) * LANES]
        for n in range(2):
            for c in range(width // LANES):
                out[n, :, c * LANES : (c + 1) * LANES] = woven[n, c]


def lane_order(rows, spin):
    size = 2 * rows * spin
    lane = lax.iota(jnp.int32, size)
    a, part, i = lane // (2 * rows), lane // rows % 2, lane % rows
    target = part * rows * spin + i * spin + a
    return (target[:, None] == lane[None, :]).astype(BF16)


def pair_contraction(blocks, own, other, pieces, scale):
    half, _, count, _ = own.shape
    spin = pieces[0][0].shape[1]
    depths = [depth for _, depth in pieces]
    total = sum(depths)
    rows = count // lax.axis_size("tile")
    order = lane_order(rows, spin)
    mixed = pltpu.VMEM((2, spin, total, 2 * rows), F32)
    return pl.pallas_call(
        functools.partial(pair_kernel, depths=depths, scale=scale),
        in_specs=[pl.BlockSpec(memory_space=pltpu.SMEM)]
        + [pl.BlockSpec(memory_space=pltpu.HBM)] * (3 + len(pieces)),
        out_specs=[pl.BlockSpec(memory_space=pltpu.VMEM)] * 2,
        out_shape=[jax.ShapeDtypeStruct((2, rows * spin, rows * spin), F32)] * 2,
        scratch_shapes=[
            mixed,
            mixed,
            pltpu.VMEM((2, rows * spin // LANES, rows * spin, LANES), F32),
            pltpu.VMEM((2, spin, total, count), F32),
            pltpu.VMEM((2 * half, 2, count, count), F32),
            pltpu.VMEM(order.shape, BF16),
            pltpu.SemaphoreType.DMA((len(pieces) + 3,)),
        ],
        compiler_params=pltpu.CompilerParams(vmem_limit_bytes=PAIR_VMEM),
        name="pair_contraction",
    )(blocks, own, other, order, *[piece for piece, _ in pieces])


def per_device(eigenvectors, perambulator, momenta, graph_blocks):
    space_count = lax.axis_size("space")
    tile_count = lax.axis_size("tile")
    space_index = lax.axis_index("space")
    tile_index = lax.axis_index("tile")
    device = space_index * tile_count + tile_index
    _, count, colours, sites = eigenvectors.shape
    order = perambulator.shape[2]
    norm = 1.0 / math.sqrt(colours * sites * space_count * tile_count)
    planes = eigenvectors.transpose(0, 2, 1, 3)

    def gram(started):
        return local_gram(planes, momenta, norm, started)

    own, other, pieces = exchange_everything(perambulator, gram)
    half = momenta.shape[0] // 2
    own = own.reshape(half, 2, count, count)
    other = other.reshape(half, 2, count, count)
    rows, columns = count // tile_count, count // space_count
    start = (0, 0, tile_index * rows, space_index * columns)
    own_part = lax.dynamic_slice(own, start, (half, 2, rows, columns))
    other_part = lax.dynamic_slice(other, start, (half, 2, rows, columns))
    elementals = jnp.where(
        tile_index % 2 == 0,
        jnp.concatenate([own_part, other_part]),
        jnp.concatenate([other_part, own_part]),
    )
    scale = 1.0 / (count * math.sqrt(order))
    blocks = jnp.stack([graph_blocks[device ^ 1], graph_blocks[device]])
    away, kept = pair_contraction(blocks, own, other, pieces, scale)
    return elementals, (kept + swap(away, "tile", 0))[None]


def solution(mesh):
    in_specs = (P(None, None, None, ("space", "tile")), P(None, "space", None), P(), P())
    out_specs = (P(None, None, "tile", "space"), P(("space", "tile"), None, None, None))
    return jax.shard_map(
        per_device, mesh=mesh, in_specs=in_specs, out_specs=out_specs, check_vma=False
    )
```

```python
import functools
import math

import jax
import jax.numpy as jnp
from jax import lax
from jax.experimental import pallas as pl
from jax.experimental.pallas import tpu as pltpu
from jax.sharding import PartitionSpec as P

LATTICE_EDGE = 64
LANES = 128
F32 = jnp.float32
BF16 = jnp.bfloat16
WAVE_ENDS = (-2, 0)
PASS_ENDS = (-1, 1, 2)
GRAM_VMEM = 55 * 1024 * 1024
PAIR_VMEM = 58 * 1024 * 1024


def bits_of(count):
    return range(count.bit_length() - 1)


def split(value):
    high = value.astype(BF16)
    return high, (value - high.astype(F32)).astype(BF16)


def dot_nt(left, right):
    return lax.dot_general(left, right, (((1,), (1,)), ((), ())), preferred_element_type=F32)


def product(left, right):
    return dot_nt(left[0], right[0]) + dot_nt(left[0], right[1]) + dot_nt(left[1], right[0])


def dot_tn(left, right):
    return lax.dot_general(left, right, (((0,), (0,)), ((), ())), preferred_element_type=F32)


def gram_kernel(momenta, vectors, *refs, width, norm):
    away, kept, held, arrived = refs[-4:]
    _, colours, _, sites = vectors.shape
    core = lax.rem(lax.axis_index("tile"), 2)
    first_site = (lax.axis_index("space") * lax.axis_size("tile") + lax.axis_index("tile")) * sites
    chunks = sites // width
    copies = []
    for colour in range(colours):
        for chunk in range(chunks):
            lanes = pl.ds(chunk * width, width)
            copies.append(
                pltpu.make_async_copy(
                    vectors.at[:, colour, :, lanes], held.at[:, colour, :, lanes], arrived.at[len(copies)]
                )
            )
    for copy in copies:
        copy.start()
    half = kept.shape[0]
    sums = []
    for total, first in ((kept, core * half), (away, (1 - core) * half)):
        for p in range(half):
            phases = []
            for chunk in range(chunks):
                site = first_site + chunk * width + lax.broadcasted_iota(jnp.int32, (1, width), 1)
                wave = (
                    momenta[first + p, 0] * (site % LATTICE_EDGE)
                    + momenta[first + p, 1] * (site // LATTICE_EDGE % LATTICE_EDGE)
                    + momenta[first + p, 2] * (site // (LATTICE_EDGE * LATTICE_EDGE))
                ) % LATTICE_EDGE
                theta = wave.astype(F32) * (2.0 * math.pi / LATTICE_EDGE)
                phases.append((jnp.cos(theta), jnp.sin(theta)))
            sums.append((total, p, phases))
    held_sums = {}
    for n, copy in enumerate(copies):
        copy.wait()
        chunk = n % chunks
        real = held[0, n // chunks, :, chunk * width : (chunk + 1) * width]
        imag = held[1, n // chunks, :, chunk * width : (chunk + 1) * width]
        left = split(real), split(imag), split(real - imag)
        for number, (_, _, phases) in enumerate(sums):
            cosine, sine = phases[chunk]
            phased_real = cosine * real + sine * imag
            phased_imag = cosine * imag - sine * real
            by_real = product(left[2], split(phased_real))
            from_real = product(left[0], split(phased_imag - phased_real))
            from_imag = product(left[1], split(phased_real + phased_imag))
            parts = by_real, from_real, from_imag
            held_sums[number] = parts if n == 0 else [old + new for old, new in zip(held_sums[number], parts)]
    for number, (total, p, _) in enumerate(sums):
        by_real, from_real, from_imag = held_sums[number]
        total[p, 0] = (by_real + from_imag) * norm
        total[p, 1] = (by_real + from_real) * norm


def local_gram(planes, momenta, norm, started):
    _, colours, count, sites = planes.shape
    half = momenta.shape[0] // 2
    width = min(sites, 512)
    return pl.pallas_call(
        functools.partial(gram_kernel, width=width, norm=norm),
        in_specs=[pl.BlockSpec(memory_space=pltpu.SMEM), pl.BlockSpec(memory_space=pltpu.HBM)]
        + [pl.BlockSpec(memory_space=pl.ANY)] * len(started),
        out_specs=[pl.BlockSpec(memory_space=pltpu.VMEM)] * 2,
        out_shape=[jax.ShapeDtypeStruct((half, 2, count, count), F32)] * 2,
        scratch_shapes=[
            pltpu.VMEM(planes.shape, F32),
            pltpu.SemaphoreType.DMA((colours * sites // width,)),
        ],
        compiler_params=pltpu.CompilerParams(vmem_limit_bytes=GRAM_VMEM),
        cost_estimate=pl.CostEstimate(
            flops=48 * half * count * count * colours * sites,
            bytes_accessed=8 * count * colours * sites,
            transcendentals=0,
        ),
        name="local_gram",
    )(momenta, planes, *started)


def together(*values):
    anywhere = pl.BlockSpec(memory_space=pl.ANY)
    return pl.pallas_call(
        lambda *refs: None,
        in_specs=[anywhere] * len(values),
        out_specs=[anywhere] * len(values),
        out_shape=[jax.ShapeDtypeStruct(value.shape, value.dtype) for value in values],
        input_output_aliases={n: n for n in range(len(values))},
        compiler_params=pltpu.CompilerParams(vmem_limit_bytes=1024 * 1024),
        name="together",
    )(*values)


def swap(value, axis, bit):
    size = lax.axis_size(axis)
    return lax.ppermute(value, axis, [(i, i ^ (1 << bit)) for i in range(size)])


def shift(value, axis, by):
    size = lax.axis_size(axis)
    return lax.ppermute(value, axis, [(i, i + by) for i in range(size) if 0 <= i + by < size])


def own_bit(axis, bit):
    return (lax.axis_index(axis) >> bit) & 1


def halve(value, axis, bit):
    mine = own_bit(axis, bit)
    half = value.shape[0] // 2
    away = lax.dynamic_slice_in_dim(value, (1 - mine) * half, half, 0)
    kept = lax.dynamic_slice_in_dim(value, mine * half, half, 0)
    return kept + swap(away, axis, bit)


def both(value, axis, bit):
    return value + swap(value, axis, bit)


def double(value, axis, bit):
    other = swap(value, axis, bit)
    return jnp.where(
        own_bit(axis, bit) == 0,
        jnp.concatenate([value, other]),
        jnp.concatenate([other, value]),
    )


def deal_kernel(tau, travel, rest, fetched, arrived, *, by_core, by_tile, tiles):
    parts, spin, _, count = travel.shape
    tile = lax.axis_index("tile")
    core = lax.rem(tile, 2)
    groups = [(pl.multiple_of(core * by_core, 8), by_core, travel, 0)]
    shared = 2 * by_core
    if by_tile:
        for n in range(tiles // 2):
            first = pl.multiple_of(shared + (2 * n + core) * by_tile, 8)
            groups.append((first, by_tile, rest, n * by_tile))
    copies, top = [], 0
    for part in range(parts):
        for first, depth, *_ in groups:
            copies.append(
                pltpu.make_async_copy(
                    tau.at[part, pl.ds(first, depth)], fetched.at[pl.ds(top, depth)], arrived.at[len(copies)]
                )
            )
            top += depth
    for copy in copies:
        copy.start()
    for copy in copies:
        copy.wait()
    rows = fetched[...]
    width = min(count, LANES)
    line = lax.broadcasted_iota(jnp.int32, (spin * width, spin * width), 0)
    lane = lax.broadcasted_iota(jnp.int32, (spin * width, spin * width), 1)
    order = (line == lane % width * spin + lane // width).astype(BF16)
    blocks = count // width
    value = jnp.concatenate(
        [rows[:, block * spin * width : (block + 1) * spin * width] for block in range(blocks)], axis=0
    )
    high = value.astype(BF16)
    middle, low = split(value - high.astype(F32))
    moved = jnp.dot(jnp.concatenate([high, middle, low], axis=0), order, preferred_element_type=F32)
    size = value.shape[0]
    moved = moved[:size] + moved[size : 2 * size] + moved[2 * size :]
    top = 0
    for block in range(blocks):
        for part in range(parts):
            for _, depth, target, at in groups:
                for a in range(spin):
                    target[part, a, at : at + depth, block * width : (block + 1) * width] = moved[
                        top : top + depth, a * width : (a + 1) * width
                    ]
                top += depth
    if by_tile:
        mine = pl.ds(pl.multiple_of(tile // 2 * by_tile, 8), by_tile)
        for part in range(parts):
            for a in range(spin):
                travel[part, a, by_core : by_core + by_tile, :] = rest[part, a, mine, :]


def deal(part, spin, by_core, by_tile):
    parts, _, order = part.shape
    tiles = lax.axis_size("tile")
    shape = (parts, spin, by_core + by_tile, order // spin)
    rest = (parts, spin, max(tiles // 2 * by_tile, 8), order // spin)
    return pl.pallas_call(
        functools.partial(deal_kernel, by_core=by_core, by_tile=by_tile, tiles=tiles),
        in_specs=[pl.BlockSpec(memory_space=pltpu.HBM)],
        out_specs=[pl.BlockSpec(memory_space=pltpu.VMEM)] * 2,
        out_shape=[jax.ShapeDtypeStruct(shape, F32), jax.ShapeDtypeStruct(rest, F32)],
        scratch_shapes=[
            pltpu.VMEM((parts * (by_core + tiles // 2 * by_tile), order), F32),
            pltpu.SemaphoreType.DMA((parts * (1 + tiles // 2),)),
        ],
        compiler_params=pltpu.CompilerParams(vmem_limit_bytes=PAIR_VMEM),
        name="deal",
    )(part)


def exchange_everything(part, gram, extra):
    space_bits, tile_bits = bits_of(lax.axis_size("space")), bits_of(lax.axis_size("tile"))
    tile_count = lax.axis_size("tile")
    sources = part.shape[1]
    shared = sources // 4
    if (sources - shared) // tile_count % 8:
        shared = sources
    by_core, by_tile = shared // 2, (sources - shared) // tile_count
    mixed, rest = deal(part, 4, by_core, by_tile)
    pieces = [(mixed, by_core)]
    if by_tile:
        pieces.append((rest, rest.shape[2]))

    slots = {0: mixed}
    places = lax.axis_size("space")

    def wave_of(mask):
        return 2 if mask == 3 else mask.bit_count() - 1

    waves = max(wave_of(mask) for mask in range(1, places)) + 1
    masks_of = [[mask for mask in range(1, places) if wave_of(mask) == w] for w in range(waves)]

    def wave(w):
        bits = [1 if mask == 3 else (mask & -mask).bit_length() - 1 for mask in masks_of[w]]
        return [swap(slots[mask ^ (1 << bit)], "space", bit) for mask, bit in zip(masks_of[w], bits)]

    def passing(w):
        arrived = []
        if by_tile:
            held = jnp.concatenate([slots[mask][:, :, by_core:] for mask in masks_of[w]], axis=2)
            for bit in tile_bits[1:]:
                arrived.append(swap(held, "tile", bit))
                held = jnp.concatenate([held, arrived[-1]], axis=2)
        return arrived

    coming = {}

    def land(rows, step):
        landing = [w for w in range(waves) if wave_end(w) == step]
        values = [coming.pop(("wave", w)) for w in landing]
        passed = [coming.pop(("pass", w)) for w in range(waves) if pass_end(w) == step]
        flat = [piece for group in values + passed for piece in group]
        if flat:
            rows, *flat = together(rows, *flat)
            pieces.extend((piece, piece.shape[2]) for piece in flat)
            for w in landing:
                slots.update(zip(masks_of[w], flat))
                flat = flat[len(masks_of[w]) :]
        for w in landing:
            if w + 1 < waves:
                coming["wave", w + 1] = wave(w + 1)
            coming["pass", w] = passing(w)
        return rows

    steps = [(halve, "tile", b) for b in tile_bits[1:]]
    steps += [(halve, "space", b) for b in space_bits[:1]]
    steps += [(both, "space", b) for b in space_bits[1:]]
    middle = len(steps) - 2
    steps += [(double, axis, b) for step, axis, b in steps[::-1] if step is halve]

    def wave_end(w):
        return -1 if w == 0 else middle + WAVE_ENDS[w - 1] if w <= len(WAVE_ENDS) else len(steps) + w

    def pass_end(w):
        return middle + PASS_ENDS[w] if w < len(PASS_ENDS) else len(steps) + waves + w

    coming["wave", 0] = wave(0)
    away, kept = gram([mixed])
    away = land(away.reshape(-1, kept.shape[-1]), -1)
    rows = kept.reshape(-1, kept.shape[-1]) + swap(away, "tile", 0)
    for n, (step, axis, bit) in enumerate(steps):
        rows = step(rows, axis, bit)
        if n == middle - 1:
            rows, *extra = together(rows, *extra)
        rows = land(rows, n)
    for n in range(len(steps), len(steps) + 2 * waves):
        rows = land(rows, n)
    return rows, swap(rows, "tile", 0), pieces, extra


def pair_kernel(blocks, own, other, order, *refs, depths, scale):
    sources = refs[: len(depths)]
    away, kept, part_out, left, right, woven, tau, held, placing, arrived = refs[len(depths) :]
    _, spin, total, count = tau.shape
    outs = (away, kept)
    rows = left.shape[3] // 2
    tiles = count // rows
    half = own.shape[0]
    core = lax.rem(lax.axis_index("tile"), 2)
    gathered = [
        pltpu.make_async_copy(own, held.at[pl.ds(core * half, half)], arrived.at[len(depths)]),
        pltpu.make_async_copy(other, held.at[pl.ds((1 - core) * half, half)], arrived.at[len(depths) + 1]),
    ]
    copies, first = [], 0
    for n, depth in enumerate(depths):
        target = tau.at[:, :, pl.ds(first, depth)]
        copies.append(pltpu.make_async_copy(sources[n].at[:, :, pl.ds(0, depth)], target, arrived.at[n]))
        first += depth
    last = pltpu.make_async_copy(order, placing, arrived.at[len(depths) + 2])
    for copy in [*gathered, *copies, last]:
        copy.start()
    for copy in gathered:
        copy.wait()
    real_rows, imag_rows = [], []
    for side in range(4):
        block = blocks[side // 2, side % 2]
        p = block // tiles
        start = pl.multiple_of(block % tiles * rows, rows)
        real = held[p, 0, pl.ds(start, rows), :]
        imag = held[p, 1, pl.ds(start, rows), :]
        real_rows += [real, imag]
        imag_rows += [-imag, real]
    weights = split(
        jnp.concatenate([jnp.concatenate(real_rows, axis=0), jnp.concatenate(imag_rows, axis=0)], axis=1)
    )
    columns = part_out.shape[3]
    line = lax.broadcasted_iota(jnp.int32, (count, columns), 0)
    lane = lax.broadcasted_iota(jnp.int32, (count, columns), 1)
    chosen = (line == lane + lax.axis_index("space") * columns).astype(BF16)
    mine = pl.ds(pl.multiple_of(lax.axis_index("tile") * rows, rows), rows)
    for p in range(2 * half):
        for part in range(2):
            value = held[p, part, mine, :]
            high = value.astype(BF16)
            middle, low = split(value - high.astype(F32))
            part_out[p, part] = (
                jnp.dot(high, chosen, preferred_element_type=F32)
                + jnp.dot(middle, chosen, preferred_element_type=F32)
            ) + jnp.dot(low, chosen, preferred_element_type=F32)
    depth = min(total, 256)
    for n in range(total // depth):
        while copies and sum(depths[: len(depths) - len(copies)]) < (n + 1) * depth:
            copies.pop(0).wait()
        here = pl.ds(n * depth, depth)

        def mix(a, carry):
            given = jnp.concatenate([tau[0, a, here, :], tau[1, a, here, :]], axis=1)
            mixed = product(split(given), weights)
            for g in range(2):
                left[g, a, here, :] = mixed[:, 4 * g * rows : (4 * g + 2) * rows]
                right[g, a, here, :] = mixed[:, (4 * g + 2) * rows : (4 * g + 4) * rows]
            return carry

        for a in range(spin):
            mix(a, 0)
    last.wait()
    width = rows * spin
    for g, out in enumerate(outs):
        left_hi, left_lo = split(jnp.concatenate([left[g, a] for a in range(spin)], axis=1))
        right_hi, right_lo = split(jnp.concatenate([right[g, a] for a in range(spin)], axis=1))
        pair = (dot_tn(left_hi, right_hi) + dot_tn(left_hi, right_lo) + dot_tn(left_lo, right_hi)) * scale
        top = jnp.concatenate([pair[2 * a * rows : (2 * a + 1) * rows] for a in range(spin)], axis=0)
        low = jnp.concatenate([pair[(2 * a + 1) * rows : (2 * a + 2) * rows] for a in range(spin)], axis=0)
        lane = lax.broadcasted_iota(jnp.int32, top.shape, 1)
        swapped = jnp.concatenate(
            [pltpu.roll(low[:, 2 * a * rows : 2 * (a + 1) * rows], rows, 1) for a in range(spin)], axis=1
        )
        pair = top + jnp.where(lane % (2 * rows) < rows, -swapped, swapped)
        pair_hi, pair_lo = split(pair)
        placed = jnp.dot(pair_hi, placing[...], preferred_element_type=F32) + jnp.dot(
            pair_lo, placing[...], preferred_element_type=F32
        )
        for a in range(spin):
            for n in range(2):
                value = placed[a * rows : (a + 1) * rows, n * width : (n + 1) * width]
                for c in range(width // LANES):
                    woven[n, c, pl.ds(a, rows, stride=spin), :] = value[:, c * LANES : (c + 1) * LANES]
        for n in range(2):
            for c in range(width // LANES):
                out[n, :, c * LANES : (c + 1) * LANES] = woven[n, c]


def lane_order(rows, spin):
    size = 2 * rows * spin
    lane = lax.iota(jnp.int32, size)
    a, part, i = lane // (2 * rows), lane // rows % 2, lane % rows
    target = part * rows * spin + i * spin + a
    return (target[:, None] == lane[None, :]).astype(BF16)


def pair_contraction(blocks, order, own, other, pieces, scale):
    half, _, count, _ = own.shape
    spin = pieces[0][0].shape[1]
    depths = [depth for _, depth in pieces]
    total = sum(depths)
    rows = count // lax.axis_size("tile")
    mixed = pltpu.VMEM((2, spin, total, 2 * rows), F32)
    return pl.pallas_call(
        functools.partial(pair_kernel, depths=depths, scale=scale),
        in_specs=[pl.BlockSpec(memory_space=pltpu.SMEM)]
        + [pl.BlockSpec(memory_space=pltpu.HBM)] * (3 + len(pieces)),
        out_specs=[pl.BlockSpec(memory_space=pltpu.VMEM)] * 3,
        out_shape=[jax.ShapeDtypeStruct((2, rows * spin, rows * spin), F32)] * 2
        + [jax.ShapeDtypeStruct((2 * half, 2, rows, count // lax.axis_size("space")), F32)],
        scratch_shapes=[
            mixed,
            mixed,
            pltpu.VMEM((2, rows * spin // LANES, rows * spin, LANES), F32),
            pltpu.VMEM((2, spin, total, count), F32),
            pltpu.VMEM((2 * half, 2, count, count), F32),
            pltpu.VMEM(order.shape, BF16),
            pltpu.SemaphoreType.DMA((len(pieces) + 3,)),
        ],
        compiler_params=pltpu.CompilerParams(vmem_limit_bytes=PAIR_VMEM),
        name="pair_contraction",
    )(blocks, own, other, order, *[piece for piece, _ in pieces])


def per_device(eigenvectors, perambulator, momenta, graph_blocks):
    space_count = lax.axis_size("space")
    tile_count = lax.axis_size("tile")
    space_index = lax.axis_index("space")
    tile_index = lax.axis_index("tile")
    device = space_index * tile_count + tile_index
    _, count, colours, sites = eigenvectors.shape
    order = perambulator.shape[2]
    norm = 1.0 / math.sqrt(colours * sites * space_count * tile_count)
    planes = eigenvectors.transpose(0, 2, 1, 3)

    def gram(started):
        return local_gram(planes, momenta, norm, started)

    spin = order // count
    blocks = jnp.stack([graph_blocks[device ^ 1], graph_blocks[device]])
    extra = [blocks, lane_order(count // tile_count, spin)]
    own, other, pieces, extra = exchange_everything(perambulator, gram, extra)
    half = momenta.shape[0] // 2
    own = own.reshape(half, 2, count, count)
    other = other.reshape(half, 2, count, count)
    scale = 1.0 / (count * math.sqrt(order))
    away, kept, elementals = pair_contraction(*extra, own, other, pieces, scale)
    return elementals, (kept + swap(away, "tile", 0))[None]


def solution(mesh):
    in_specs = (P(None, None, None, ("space", "tile")), P(None, "space", None), P(), P())
    out_specs = (P(None, None, "tile", "space"), P(("space", "tile"), None, None, None))
    return jax.shard_map(
        per_device, mesh=mesh, in_specs=in_specs, out_specs=out_specs, check_vma=False
    )
```

```python
import functools
import math

import jax
import jax.numpy as jnp
from jax import lax
from jax.experimental import pallas as pl
from jax.experimental.pallas import tpu as pltpu
from jax.sharding import PartitionSpec as P

LATTICE_EDGE = 64
LANES = 128
F32 = jnp.float32
BF16 = jnp.bfloat16
WAVE_ENDS = (-2, 0)
PASS_ENDS = (-1, 1, 2)
GRAM_VMEM = 55 * 1024 * 1024
PAIR_VMEM = 58 * 1024 * 1024


def bits_of(count):
    return range(count.bit_length() - 1)


def split(value):
    high = value.astype(BF16)
    return high, (value - high.astype(F32)).astype(BF16)


def dot_nt(left, right):
    return lax.dot_general(left, right, (((1,), (1,)), ((), ())), preferred_element_type=F32)


def product(left, right):
    return dot_nt(left[0], right[0]) + dot_nt(left[0], right[1]) + dot_nt(left[1], right[0])


def dot_tn(left, right):
    return lax.dot_general(left, right, (((0,), (0,)), ((), ())), preferred_element_type=F32)


def gram_kernel(momenta, vectors, *refs, width, norm):
    away, kept, held, arrived = refs[-4:]
    _, colours, _, sites = vectors.shape
    core = lax.rem(lax.axis_index("tile"), 2)
    first_site = (lax.axis_index("space") * lax.axis_size("tile") + lax.axis_index("tile")) * sites
    chunks = sites // width
    copies = []
    for colour in range(colours):
        for chunk in range(chunks):
            lanes = pl.ds(chunk * width, width)
            copies.append(
                pltpu.make_async_copy(
                    vectors.at[:, colour, :, lanes], held.at[:, colour, :, lanes], arrived.at[len(copies)]
                )
            )
    for copy in copies:
        copy.start()
    half = kept.shape[0]
    sums = []
    for total, first in ((kept, core * half), (away, (1 - core) * half)):
        for p in range(half):
            phases = []
            for chunk in range(chunks):
                site = first_site + chunk * width + lax.broadcasted_iota(jnp.int32, (1, width), 1)
                wave = (
                    momenta[first + p, 0] * (site % LATTICE_EDGE)
                    + momenta[first + p, 1] * (site // LATTICE_EDGE % LATTICE_EDGE)
                    + momenta[first + p, 2] * (site // (LATTICE_EDGE * LATTICE_EDGE))
                ) % LATTICE_EDGE
                theta = wave.astype(F32) * (2.0 * math.pi / LATTICE_EDGE)
                phases.append((jnp.cos(theta), jnp.sin(theta)))
            sums.append((total, p, phases))
    held_sums = {}
    for n, copy in enumerate(copies):
        copy.wait()
        chunk = n % chunks
        real = held[0, n // chunks, :, chunk * width : (chunk + 1) * width]
        imag = held[1, n // chunks, :, chunk * width : (chunk + 1) * width]
        left = split(real), split(imag), split(real - imag)
        for number, (_, _, phases) in enumerate(sums):
            cosine, sine = phases[chunk]
            phased_real = cosine * real + sine * imag
            phased_imag = cosine * imag - sine * real
            by_real = product(left[2], split(phased_real))
            from_real = product(left[0], split(phased_imag - phased_real))
            from_imag = product(left[1], split(phased_real + phased_imag))
            parts = by_real, from_real, from_imag
            held_sums[number] = parts if n == 0 else [old + new for old, new in zip(held_sums[number], parts)]
    for number, (total, p, _) in enumerate(sums):
        by_real, from_real, from_imag = held_sums[number]
        total[p, 0] = (by_real + from_imag) * norm
        total[p, 1] = (by_real + from_real) * norm


def local_gram(planes, momenta, norm, started):
    _, colours, count, sites = planes.shape
    half = momenta.shape[0] // 2
    width = min(sites, 512)
    return pl.pallas_call(
        functools.partial(gram_kernel, width=width, norm=norm),
        in_specs=[pl.BlockSpec(memory_space=pltpu.SMEM), pl.BlockSpec(memory_space=pltpu.HBM)]
        + [pl.BlockSpec(memory_space=pl.ANY)] * len(started),
        out_specs=[pl.BlockSpec(memory_space=pltpu.VMEM)] * 2,
        out_shape=[jax.ShapeDtypeStruct((half, 2, count, count), F32)] * 2,
        scratch_shapes=[
            pltpu.VMEM(planes.shape, F32),
            pltpu.SemaphoreType.DMA((colours * sites // width,)),
        ],
        compiler_params=pltpu.CompilerParams(vmem_limit_bytes=GRAM_VMEM),
        cost_estimate=pl.CostEstimate(
            flops=48 * half * count * count * colours * sites,
            bytes_accessed=8 * count * colours * sites,
            transcendentals=0,
        ),
        name="local_gram",
    )(momenta, planes, *started)


def together(*values):
    anywhere = pl.BlockSpec(memory_space=pl.ANY)
    return pl.pallas_call(
        lambda *refs: None,
        in_specs=[anywhere] * len(values),
        out_specs=[anywhere] * len(values),
        out_shape=[jax.ShapeDtypeStruct(value.shape, value.dtype) for value in values],
        input_output_aliases={n: n for n in range(len(values))},
        compiler_params=pltpu.CompilerParams(vmem_limit_bytes=1024 * 1024),
        name="together",
    )(*values)


def swap(value, axis, bit):
    size = lax.axis_size(axis)
    return lax.ppermute(value, axis, [(i, i ^ (1 << bit)) for i in range(size)])


def shift(value, axis, by):
    size = lax.axis_size(axis)
    return lax.ppermute(value, axis, [(i, i + by) for i in range(size) if 0 <= i + by < size])


def own_bit(axis, bit):
    return (lax.axis_index(axis) >> bit) & 1


def halve(value, axis, bit):
    mine = own_bit(axis, bit)
    half = value.shape[0] // 2
    away = lax.dynamic_slice_in_dim(value, (1 - mine) * half, half, 0)
    kept = lax.dynamic_slice_in_dim(value, mine * half, half, 0)
    return kept + swap(away, axis, bit)


def both(value, axis, bit):
    return value + swap(value, axis, bit)


def double(value, axis, bit):
    other = swap(value, axis, bit)
    return jnp.where(
        own_bit(axis, bit) == 0,
        jnp.concatenate([value, other]),
        jnp.concatenate([other, value]),
    )


def deal_kernel(tau, travel, whole, fetched, arrived, *, by_core, by_tile, tiles):
    parts, spin, _, count = travel.shape
    tile = lax.axis_index("tile")
    core = lax.rem(tile, 2)
    groups = [(pl.multiple_of(core * by_core, 8), by_core, whole, 0)]
    shared = 2 * by_core
    if by_tile:
        for n in range(tiles // 2):
            first = pl.multiple_of(shared + (2 * n + core) * by_tile, 8)
            groups.append((first, by_tile, whole, by_core + n * by_tile))
    copies, top = [], 0
    for part in range(parts):
        for first, depth, *_ in groups:
            copies.append(
                pltpu.make_async_copy(
                    tau.at[part, pl.ds(first, depth)], fetched.at[pl.ds(top, depth)], arrived.at[len(copies)]
                )
            )
            top += depth
    for copy in copies:
        copy.start()
    for copy in copies:
        copy.wait()
    rows = fetched[...]
    width = min(count, LANES)
    line = lax.broadcasted_iota(jnp.int32, (spin * width, spin * width), 0)
    lane = lax.broadcasted_iota(jnp.int32, (spin * width, spin * width), 1)
    order = (line == lane % width * spin + lane // width).astype(BF16)
    blocks = count // width
    value = jnp.concatenate(
        [rows[:, block * spin * width : (block + 1) * spin * width] for block in range(blocks)], axis=0
    )
    high = value.astype(BF16)
    middle, low = split(value - high.astype(F32))
    moved = jnp.dot(jnp.concatenate([high, middle, low], axis=0), order, preferred_element_type=F32)
    size = value.shape[0]
    moved = moved[:size] + moved[size : 2 * size] + moved[2 * size :]
    top = 0
    for block in range(blocks):
        for part in range(parts):
            for _, depth, target, at in groups:
                for a in range(spin):
                    target[part, a, at : at + depth, block * width : (block + 1) * width] = moved[
                        top : top + depth, a * width : (a + 1) * width
                    ]
                top += depth
    for part in range(parts):
        for a in range(spin):
            travel[part, a, :by_core, :] = whole[part, a, :by_core, :]
            if by_tile:
                mine = pl.ds(pl.multiple_of(by_core + tile // 2 * by_tile, 8), by_tile)
                travel[part, a, by_core : by_core + by_tile, :] = whole[part, a, mine, :]


def deal(part, spin, by_core, by_tile):
    parts, _, order = part.shape
    tiles = lax.axis_size("tile")
    shape = (parts, spin, by_core + by_tile, order // spin)
    whole = (parts, spin, by_core + tiles // 2 * by_tile, order // spin)
    return pl.pallas_call(
        functools.partial(deal_kernel, by_core=by_core, by_tile=by_tile, tiles=tiles),
        in_specs=[pl.BlockSpec(memory_space=pltpu.HBM)],
        out_specs=[pl.BlockSpec(memory_space=pltpu.VMEM)] * 2,
        out_shape=[jax.ShapeDtypeStruct(shape, F32), jax.ShapeDtypeStruct(whole, F32)],
        scratch_shapes=[
            pltpu.VMEM((parts * (by_core + tiles // 2 * by_tile), order), F32),
            pltpu.SemaphoreType.DMA((parts * (1 + tiles // 2),)),
        ],
        compiler_params=pltpu.CompilerParams(vmem_limit_bytes=PAIR_VMEM),
        name="deal",
    )(part)


def exchange_everything(part, gram, extra):
    space_bits, tile_bits = bits_of(lax.axis_size("space")), bits_of(lax.axis_size("tile"))
    tile_count = lax.axis_size("tile")
    sources = part.shape[1]
    shared = sources // 4
    if (sources - shared) // tile_count % 8:
        shared = sources
    by_core, by_tile = shared // 2, (sources - shared) // tile_count
    mixed, whole = deal(part, 4, by_core, by_tile)
    pieces = [(whole, whole.shape[2])]

    slots = {0: mixed}
    places = lax.axis_size("space")

    def wave_of(mask):
        return 2 if mask == 3 else mask.bit_count() - 1

    waves = max(wave_of(mask) for mask in range(1, places)) + 1
    masks_of = [[mask for mask in range(1, places) if wave_of(mask) == w] for w in range(waves)]

    def wave(w):
        bits = [1 if mask == 3 else (mask & -mask).bit_length() - 1 for mask in masks_of[w]]
        given = [whole if mask == 1 else slots[mask ^ (1 << bit)] for mask, bit in zip(masks_of[w], bits)]
        return [swap(value, "space", bit) for value, bit in zip(given, bits)]

    def passing(w):
        arrived = []
        if by_tile:
            held = jnp.concatenate([slots[mask][:, :, by_core:] for mask in masks_of[w] if mask > 1], axis=2)
            for bit in tile_bits[1:]:
                arrived.append(swap(held, "tile", bit))
                held = jnp.concatenate([held, arrived[-1]], axis=2)
        return arrived

    coming = {}

    def land(rows, step):
        landing = [w for w in range(waves) if wave_end(w) == step]
        values = [coming.pop(("wave", w)) for w in landing]
        passed = [coming.pop(("pass", w)) for w in range(waves) if pass_end(w) == step]
        flat = [piece for group in values + passed for piece in group]
        if flat:
            rows, *flat = together(rows, *flat)
            pieces.extend((piece, piece.shape[2]) for piece in flat)
            for w in landing:
                slots.update(zip(masks_of[w], flat))
                flat = flat[len(masks_of[w]) :]
            if 0 in landing and by_tile:
                first = by_core + lax.axis_index("tile") // 2 * by_tile
                mine = lax.dynamic_slice_in_dim(slots[1], first, by_tile, 2)
                slots[1] = jnp.concatenate([slots[1][:, :, :by_core], mine], axis=2)
        for w in landing:
            if w + 1 < waves:
                coming["wave", w + 1] = wave(w + 1)
            coming["pass", w] = passing(w)
        return rows

    steps = [(halve, "tile", b) for b in tile_bits[1:]]
    steps += [(halve, "space", b) for b in space_bits[:1]]
    steps += [(both, "space", b) for b in space_bits[1:]]
    middle = len(steps) - 2
    steps += [(double, axis, b) for step, axis, b in steps[::-1] if step is halve]

    def wave_end(w):
        return -1 if w == 0 else middle + WAVE_ENDS[w - 1] if w <= len(WAVE_ENDS) else len(steps) + w

    def pass_end(w):
        return middle + PASS_ENDS[w] if w < len(PASS_ENDS) else len(steps) + waves + w

    coming["wave", 0] = wave(0)
    away, kept = gram([mixed])
    away = land(away.reshape(-1, kept.shape[-1]), -1)
    rows = kept.reshape(-1, kept.shape[-1]) + swap(away, "tile", 0)
    for n, (step, axis, bit) in enumerate(steps):
        rows = step(rows, axis, bit)
        if n == middle - 1:
            rows, *extra = together(rows, *extra)
        rows = land(rows, n)
    for n in range(len(steps), len(steps) + 2 * waves):
        rows = land(rows, n)
    return rows, swap(rows, "tile", 0), pieces, extra


def pair_kernel(blocks, own, other, order, *refs, depths, scale):
    sources = refs[: len(depths)]
    away, kept, part_out, left, right, woven, tau, held, placing, arrived = refs[len(depths) :]
    _, spin, total, count = tau.shape
    outs = (away, kept)
    rows = left.shape[3] // 2
    tiles = count // rows
    half = own.shape[0]
    core = lax.rem(lax.axis_index("tile"), 2)
    gathered = [
        pltpu.make_async_copy(own, held.at[pl.ds(core * half, half)], arrived.at[len(depths)]),
        pltpu.make_async_copy(other, held.at[pl.ds((1 - core) * half, half)], arrived.at[len(depths) + 1]),
    ]
    copies, first = [], 0
    for n, depth in enumerate(depths):
        target = tau.at[:, :, pl.ds(first, depth)]
        copies.append(pltpu.make_async_copy(sources[n].at[:, :, pl.ds(0, depth)], target, arrived.at[n]))
        first += depth
    last = pltpu.make_async_copy(order, placing, arrived.at[len(depths) + 2])
    for copy in [*gathered, *copies, last]:
        copy.start()
    for copy in gathered:
        copy.wait()
    real_rows, imag_rows = [], []
    for side in range(4):
        block = blocks[side // 2, side % 2]
        p = block // tiles
        start = pl.multiple_of(block % tiles * rows, rows)
        real = held[p, 0, pl.ds(start, rows), :]
        imag = held[p, 1, pl.ds(start, rows), :]
        real_rows += [real, imag]
        imag_rows += [-imag, real]
    weights = split(
        jnp.concatenate([jnp.concatenate(real_rows, axis=0), jnp.concatenate(imag_rows, axis=0)], axis=1)
    )
    columns = part_out.shape[3]
    line = lax.broadcasted_iota(jnp.int32, (count, columns), 0)
    lane = lax.broadcasted_iota(jnp.int32, (count, columns), 1)
    chosen = (line == lane + lax.axis_index("space") * columns).astype(BF16)
    mine = pl.ds(pl.multiple_of(lax.axis_index("tile") * rows, rows), rows)
    for p in range(2 * half):
        for part in range(2):
            value = held[p, part, mine, :]
            high = value.astype(BF16)
            middle, low = split(value - high.astype(F32))
            part_out[p, part] = (
                jnp.dot(high, chosen, preferred_element_type=F32)
                + jnp.dot(middle, chosen, preferred_element_type=F32)
            ) + jnp.dot(low, chosen, preferred_element_type=F32)
    depth = min(total, 256)
    for n in range(total // depth):
        while copies and sum(depths[: len(depths) - len(copies)]) < (n + 1) * depth:
            copies.pop(0).wait()
        here = pl.ds(n * depth, depth)

        def mix(a, carry):
            given = jnp.concatenate([tau[0, a, here, :], tau[1, a, here, :]], axis=1)
            mixed = product(split(given), weights)
            for g in range(2):
                left[g, a, here, :] = mixed[:, 4 * g * rows : (4 * g + 2) * rows]
                right[g, a, here, :] = mixed[:, (4 * g + 2) * rows : (4 * g + 4) * rows]
            return carry

        for a in range(spin):
            mix(a, 0)
    last.wait()
    width = rows * spin
    for g, out in enumerate(outs):
        left_hi, left_lo = split(jnp.concatenate([left[g, a] for a in range(spin)], axis=1))
        right_hi, right_lo = split(jnp.concatenate([right[g, a] for a in range(spin)], axis=1))
        pair = (dot_tn(left_hi, right_hi) + dot_tn(left_hi, right_lo) + dot_tn(left_lo, right_hi)) * scale
        top = jnp.concatenate([pair[2 * a * rows : (2 * a + 1) * rows] for a in range(spin)], axis=0)
        low = jnp.concatenate([pair[(2 * a + 1) * rows : (2 * a + 2) * rows] for a in range(spin)], axis=0)
        lane = lax.broadcasted_iota(jnp.int32, top.shape, 1)
        swapped = jnp.concatenate(
            [pltpu.roll(low[:, 2 * a * rows : 2 * (a + 1) * rows], rows, 1) for a in range(spin)], axis=1
        )
        pair = top + jnp.where(lane % (2 * rows) < rows, -swapped, swapped)
        pair_hi, pair_lo = split(pair)
        placed = jnp.dot(pair_hi, placing[...], preferred_element_type=F32) + jnp.dot(
            pair_lo, placing[...], preferred_element_type=F32
        )
        for a in range(spin):
            for n in range(2):
                value = placed[a * rows : (a + 1) * rows, n * width : (n + 1) * width]
                for c in range(width // LANES):
                    woven[n, c, pl.ds(a, rows, stride=spin), :] = value[:, c * LANES : (c + 1) * LANES]
        for n in range(2):
            for c in range(width // LANES):
                out[n, :, c * LANES : (c + 1) * LANES] = woven[n, c]


def lane_order(rows, spin):
    size = 2 * rows * spin
    lane = lax.iota(jnp.int32, size)
    a, part, i = lane // (2 * rows), lane // rows % 2, lane % rows
    target = part * rows * spin + i * spin + a
    return (target[:, None] == lane[None, :]).astype(BF16)


def pair_contraction(blocks, order, own, other, pieces, scale):
    half, _, count, _ = own.shape
    spin = pieces[0][0].shape[1]
    depths = [depth for _, depth in pieces]
    total = sum(depths)
    rows = count // lax.axis_size("tile")
    mixed = pltpu.VMEM((2, spin, total, 2 * rows), F32)
    return pl.pallas_call(
        functools.partial(pair_kernel, depths=depths, scale=scale),
        in_specs=[pl.BlockSpec(memory_space=pltpu.SMEM)]
        + [pl.BlockSpec(memory_space=pltpu.HBM)] * (3 + len(pieces)),
        out_specs=[pl.BlockSpec(memory_space=pltpu.VMEM)] * 3,
        out_shape=[jax.ShapeDtypeStruct((2, rows * spin, rows * spin), F32)] * 2
        + [jax.ShapeDtypeStruct((2 * half, 2, rows, count // lax.axis_size("space")), F32)],
        scratch_shapes=[
            mixed,
            mixed,
            pltpu.VMEM((2, rows * spin // LANES, rows * spin, LANES), F32),
            pltpu.VMEM((2, spin, total, count), F32),
            pltpu.VMEM((2 * half, 2, count, count), F32),
            pltpu.VMEM(order.shape, BF16),
            pltpu.SemaphoreType.DMA((len(pieces) + 3,)),
        ],
        compiler_params=pltpu.CompilerParams(vmem_limit_bytes=PAIR_VMEM),
        name="pair_contraction",
    )(blocks, own, other, order, *[piece for piece, _ in pieces])


def per_device(eigenvectors, perambulator, momenta, graph_blocks):
    space_count = lax.axis_size("space")
    tile_count = lax.axis_size("tile")
    space_index = lax.axis_index("space")
    tile_index = lax.axis_index("tile")
    device = space_index * tile_count + tile_index
    _, count, colours, sites = eigenvectors.shape
    order = perambulator.shape[2]
    norm = 1.0 / math.sqrt(colours * sites * space_count * tile_count)
    planes = eigenvectors.transpose(0, 2, 1, 3)

    def gram(started):
        return local_gram(planes, momenta, norm, started)

    spin = order // count
    blocks = jnp.stack([graph_blocks[device ^ 1], graph_blocks[device]])
    extra = [blocks, lane_order(count // tile_count, spin)]
    own, other, pieces, extra = exchange_everything(perambulator, gram, extra)
    half = momenta.shape[0] // 2
    own = own.reshape(half, 2, count, count)
    other = other.reshape(half, 2, count, count)
    scale = 1.0 / (count * math.sqrt(order))
    away, kept, elementals = pair_contraction(*extra, own, other, pieces, scale)
    return elementals, (kept + swap(away, "tile", 0))[None]


def solution(mesh):
    in_specs = (P(None, None, None, ("space", "tile")), P(None, "space", None), P(), P())
    out_specs = (P(None, None, "tile", "space"), P(("space", "tile"), None, None, None))
    return jax.shard_map(
        per_device, mesh=mesh, in_specs=in_specs, out_specs=out_specs, check_vma=False
    )
```

```python
import functools
import math

import jax
import jax.numpy as jnp
from jax import lax
from jax.experimental import pallas as pl
from jax.experimental.pallas import tpu as pltpu
from jax.sharding import PartitionSpec as P

LATTICE_EDGE = 64
LANES = 128
F32 = jnp.float32
BF16 = jnp.bfloat16
WAVE_ENDS = (-2, 0)
PASS_ENDS = (-1, 1, 2)
GRAM_VMEM = 53 * 1024 * 1024
PAIR_VMEM = 48 * 1024 * 1024


def bits_of(count):
    return range(count.bit_length() - 1)


def split(value):
    high = value.astype(BF16)
    return high, (value - high.astype(F32)).astype(BF16)


def dot_nt(left, right):
    return lax.dot_general(left, right, (((1,), (1,)), ((), ())), preferred_element_type=F32)


def product(left, right):
    return dot_nt(left[0], right[0]) + dot_nt(left[0], right[1]) + dot_nt(left[1], right[0])


def dot_tn(left, right):
    return lax.dot_general(left, right, (((0,), (0,)), ((), ())), preferred_element_type=F32)


def gram_kernel(momenta, vectors, *refs, width, norm):
    away, kept, held, arrived = refs[-4:]
    _, colours, _, sites = vectors.shape
    core = lax.rem(lax.axis_index("tile"), 2)
    first_site = (lax.axis_index("space") * lax.axis_size("tile") + lax.axis_index("tile")) * sites
    chunks = sites // width
    copies = []
    for colour in range(colours):
        for chunk in range(chunks):
            lanes = pl.ds(chunk * width, width)
            copies.append(
                pltpu.make_async_copy(
                    vectors.at[:, colour, :, lanes], held.at[:, colour, :, lanes], arrived.at[len(copies)]
                )
            )
    for copy in copies:
        copy.start()
    half = kept.shape[0]
    sums = []
    for total, first in ((kept, core * half), (away, (1 - core) * half)):
        for p in range(half):
            phases = []
            for chunk in range(chunks):
                site = first_site + chunk * width + lax.broadcasted_iota(jnp.int32, (1, width), 1)
                wave = (
                    momenta[first + p, 0] * (site % LATTICE_EDGE)
                    + momenta[first + p, 1] * (site // LATTICE_EDGE % LATTICE_EDGE)
                    + momenta[first + p, 2] * (site // (LATTICE_EDGE * LATTICE_EDGE))
                ) % LATTICE_EDGE
                theta = wave.astype(F32) * (2.0 * math.pi / LATTICE_EDGE)
                phases.append((jnp.cos(theta), jnp.sin(theta)))
            sums.append((total, p, phases))
    held_sums = {}
    for n, copy in enumerate(copies):
        copy.wait()
        chunk = n % chunks
        real = held[0, n // chunks, :, chunk * width : (chunk + 1) * width]
        imag = held[1, n // chunks, :, chunk * width : (chunk + 1) * width]
        left = split(real), split(imag), split(real - imag)
        for number, (_, _, phases) in enumerate(sums):
            cosine, sine = phases[chunk]
            phased_real = cosine * real + sine * imag
            phased_imag = cosine * imag - sine * real
            by_real = product(left[2], split(phased_real))
            from_real = product(left[0], split(phased_imag - phased_real))
            from_imag = product(left[1], split(phased_real + phased_imag))
            parts = by_real, from_real, from_imag
            held_sums[number] = parts if n == 0 else [old + new for old, new in zip(held_sums[number], parts)]
    for number, (total, p, _) in enumerate(sums):
        by_real, from_real, from_imag = held_sums[number]
        total[p, 0] = (by_real + from_imag) * norm
        total[p, 1] = (by_real + from_real) * norm


def local_gram(planes, momenta, norm, started):
    _, colours, count, sites = planes.shape
    half = momenta.shape[0] // 2
    width = min(sites, 512)
    return pl.pallas_call(
        functools.partial(gram_kernel, width=width, norm=norm),
        in_specs=[pl.BlockSpec(memory_space=pltpu.SMEM), pl.BlockSpec(memory_space=pltpu.HBM)]
        + [pl.BlockSpec(memory_space=pl.ANY)] * len(started),
        out_specs=[pl.BlockSpec(memory_space=pltpu.VMEM)] * 2,
        out_shape=[jax.ShapeDtypeStruct((half, 2, count, count), F32)] * 2,
        scratch_shapes=[
            pltpu.VMEM(planes.shape, F32),
            pltpu.SemaphoreType.DMA((colours * sites // width,)),
        ],
        compiler_params=pltpu.CompilerParams(vmem_limit_bytes=GRAM_VMEM),
        cost_estimate=pl.CostEstimate(
            flops=48 * half * count * count * colours * sites,
            bytes_accessed=8 * count * colours * sites,
            transcendentals=0,
        ),
        name="local_gram",
    )(momenta, planes, *started)


def together(*values):
    anywhere = pl.BlockSpec(memory_space=pl.ANY)
    return pl.pallas_call(
        lambda *refs: None,
        in_specs=[anywhere] * len(values),
        out_specs=[anywhere] * len(values),
        out_shape=[jax.ShapeDtypeStruct(value.shape, value.dtype) for value in values],
        input_output_aliases={n: n for n in range(len(values))},
        compiler_params=pltpu.CompilerParams(vmem_limit_bytes=1024 * 1024),
        name="together",
    )(*values)


def swap(value, axis, bit):
    size = lax.axis_size(axis)
    return lax.ppermute(value, axis, [(i, i ^ (1 << bit)) for i in range(size)])


def shift(value, axis, by):
    size = lax.axis_size(axis)
    return lax.ppermute(value, axis, [(i, i + by) for i in range(size) if 0 <= i + by < size])


def own_bit(axis, bit):
    return (lax.axis_index(axis) >> bit) & 1


def halve(value, axis, bit):
    mine = own_bit(axis, bit)
    half = value.shape[0] // 2
    away = lax.dynamic_slice_in_dim(value, (1 - mine) * half, half, 0)
    kept = lax.dynamic_slice_in_dim(value, mine * half, half, 0)
    return kept + swap(away, axis, bit)


def both(value, axis, bit):
    return value + swap(value, axis, bit)


def double(value, axis, bit):
    other = swap(value, axis, bit)
    return jnp.where(
        own_bit(axis, bit) == 0,
        jnp.concatenate([value, other]),
        jnp.concatenate([other, value]),
    )


def deal_kernel(tau, travel, whole, fetched, arrived, *, by_core, by_tile, tiles):
    parts, spin, _, count = travel.shape
    tile = lax.axis_index("tile")
    core = lax.rem(tile, 2)
    groups = [(pl.multiple_of(core * by_core, 8), by_core, whole, 0)]
    shared = 2 * by_core
    if by_tile:
        for n in range(tiles // 2):
            first = pl.multiple_of(shared + (2 * n + core) * by_tile, 8)
            groups.append((first, by_tile, whole, by_core + n * by_tile))
    copies, top = [], 0
    for part in range(parts):
        for first, depth, *_ in groups:
            copies.append(
                pltpu.make_async_copy(
                    tau.at[part, pl.ds(first, depth)], fetched.at[pl.ds(top, depth)], arrived.at[len(copies)]
                )
            )
            top += depth
    for copy in copies:
        copy.start()
    for copy in copies:
        copy.wait()
    rows = fetched[...]
    width = min(count, LANES)
    line = lax.broadcasted_iota(jnp.int32, (spin * width, spin * width), 0)
    lane = lax.broadcasted_iota(jnp.int32, (spin * width, spin * width), 1)
    order = (line == lane % width * spin + lane // width).astype(BF16)
    blocks = count // width
    value = jnp.concatenate(
        [rows[:, block * spin * width : (block + 1) * spin * width] for block in range(blocks)], axis=0
    )
    high = value.astype(BF16)
    middle, low = split(value - high.astype(F32))
    moved = jnp.dot(jnp.concatenate([high, middle, low], axis=0), order, preferred_element_type=F32)
    size = value.shape[0]
    moved = moved[:size] + moved[size : 2 * size] + moved[2 * size :]
    top = 0
    for block in range(blocks):
        for part in range(parts):
            for _, depth, target, at in groups:
                for a in range(spin):
                    target[part, a, at : at + depth, block * width : (block + 1) * width] = moved[
                        top : top + depth, a * width : (a + 1) * width
                    ]
                top += depth
    for part in range(parts):
        for a in range(spin):
            travel[part, a, :by_core, :] = whole[part, a, :by_core, :]
            if by_tile:
                mine = pl.ds(pl.multiple_of(by_core + tile // 2 * by_tile, 8), by_tile)
                travel[part, a, by_core : by_core + by_tile, :] = whole[part, a, mine, :]


def deal(part, spin, by_core, by_tile):
    parts, _, order = part.shape
    tiles = lax.axis_size("tile")
    shape = (parts, spin, by_core + by_tile, order // spin)
    whole = (parts, spin, by_core + tiles // 2 * by_tile, order // spin)
    return pl.pallas_call(
        functools.partial(deal_kernel, by_core=by_core, by_tile=by_tile, tiles=tiles),
        in_specs=[pl.BlockSpec(memory_space=pltpu.HBM)],
        out_specs=[pl.BlockSpec(memory_space=pltpu.VMEM)] * 2,
        out_shape=[jax.ShapeDtypeStruct(shape, F32), jax.ShapeDtypeStruct(whole, F32)],
        scratch_shapes=[
            pltpu.VMEM((parts * (by_core + tiles // 2 * by_tile), order), F32),
            pltpu.SemaphoreType.DMA((parts * (1 + tiles // 2),)),
        ],
        compiler_params=pltpu.CompilerParams(vmem_limit_bytes=PAIR_VMEM),
        name="deal",
    )(part)


def exchange_everything(part, gram, extra):
    space_bits, tile_bits = bits_of(lax.axis_size("space")), bits_of(lax.axis_size("tile"))
    tile_count = lax.axis_size("tile")
    sources = part.shape[1]
    shared = sources // 4
    if (sources - shared) // tile_count % 8:
        shared = sources
    by_core, by_tile = shared // 2, (sources - shared) // tile_count
    mixed, whole = deal(part, 4, by_core, by_tile)
    pieces = [(whole, whole.shape[2])]

    slots = {0: mixed}
    places = lax.axis_size("space")

    def wave_of(mask):
        return 2 if mask == 3 else mask.bit_count() - 1

    waves = max(wave_of(mask) for mask in range(1, places)) + 1
    masks_of = [[mask for mask in range(1, places) if wave_of(mask) == w] for w in range(waves)]

    def wave(w):
        bits = [1 if mask == 3 else (mask & -mask).bit_length() - 1 for mask in masks_of[w]]
        given = [whole if mask == 1 else slots[mask ^ (1 << bit)] for mask, bit in zip(masks_of[w], bits)]
        return [swap(value, "space", bit) for value, bit in zip(given, bits)]

    def passing(w):
        arrived = []
        if by_tile:
            held = jnp.concatenate([slots[mask][:, :, by_core:] for mask in masks_of[w] if mask > 1], axis=2)
            for bit in tile_bits[1:]:
                arrived.append(swap(held, "tile", bit))
                held = jnp.concatenate([held, arrived[-1]], axis=2)
        return arrived

    coming = {}

    def land(rows, step):
        landing = [w for w in range(waves) if wave_end(w) == step]
        values = [coming.pop(("wave", w)) for w in landing]
        passed = [coming.pop(("pass", w)) for w in range(waves) if pass_end(w) == step]
        flat = [piece for group in values + passed for piece in group]
        if flat:
            rows, *flat = together(rows, *flat)
            pieces.extend((piece, piece.shape[2]) for piece in flat)
            for w in landing:
                slots.update(zip(masks_of[w], flat))
                flat = flat[len(masks_of[w]) :]
            if 0 in landing and by_tile:
                first = by_core + lax.axis_index("tile") // 2 * by_tile
                mine = lax.dynamic_slice_in_dim(slots[1], first, by_tile, 2)
                slots[1] = jnp.concatenate([slots[1][:, :, :by_core], mine], axis=2)
        for w in landing:
            if w + 1 < waves:
                coming["wave", w + 1] = wave(w + 1)
            coming["pass", w] = passing(w)
        return rows

    steps = [(halve, "tile", b) for b in tile_bits[1:]]
    steps += [(halve, "space", b) for b in space_bits[:1]]
    steps += [(both, "space", b) for b in space_bits[1:]]
    middle = len(steps) - 2
    steps += [(double, axis, b) for step, axis, b in steps[::-1] if step is halve]

    def wave_end(w):
        return -1 if w == 0 else middle + WAVE_ENDS[w - 1] if w <= len(WAVE_ENDS) else len(steps) + w

    def pass_end(w):
        return middle + PASS_ENDS[w] if w < len(PASS_ENDS) else len(steps) + waves + w

    coming["wave", 0] = wave(0)
    away, kept = gram([mixed])
    away = land(away.reshape(-1, kept.shape[-1]), -1)
    rows = kept.reshape(-1, kept.shape[-1]) + swap(away, "tile", 0)
    for n, (step, axis, bit) in enumerate(steps):
        rows = step(rows, axis, bit)
        if n == middle - 1:
            rows, *extra = together(rows, *extra)
        rows = land(rows, n)
    for n in range(len(steps), len(steps) + 2 * waves):
        rows = land(rows, n)
    return rows, swap(rows, "tile", 0), pieces, extra


def pair_kernel(blocks, own, other, order, *refs, depths, scale):
    sources = refs[: len(depths)]
    away, kept, part_out, left, right, woven, tau, held, placing, arrived = refs[len(depths) :]
    _, spin, total, count = tau.shape
    outs = (away, kept)
    rows = left.shape[3] // 2
    tiles = count // rows
    half = own.shape[0]
    core = lax.rem(lax.axis_index("tile"), 2)
    gathered = [
        pltpu.make_async_copy(own, held.at[pl.ds(core * half, half)], arrived.at[len(depths)]),
        pltpu.make_async_copy(other, held.at[pl.ds((1 - core) * half, half)], arrived.at[len(depths) + 1]),
    ]
    copies, first = [], 0
    for n, depth in enumerate(depths):
        target = tau.at[:, :, pl.ds(first, depth)]
        copies.append(pltpu.make_async_copy(sources[n].at[:, :, pl.ds(0, depth)], target, arrived.at[n]))
        first += depth
    last = pltpu.make_async_copy(order, placing, arrived.at[len(depths) + 2])
    for copy in [*gathered, *copies, last]:
        copy.start()
    for copy in gathered:
        copy.wait()
    real_rows, imag_rows = [], []
    for side in range(4):
        block = blocks[side // 2, side % 2]
        p = block // tiles
        start = pl.multiple_of(block % tiles * rows, rows)
        real = held[p, 0, pl.ds(start, rows), :]
        imag = held[p, 1, pl.ds(start, rows), :]
        real_rows += [real, imag]
        imag_rows += [-imag, real]
    weights = split(
        jnp.concatenate([jnp.concatenate(real_rows, axis=0), jnp.concatenate(imag_rows, axis=0)], axis=1)
    )
    columns = part_out.shape[3]
    line = lax.broadcasted_iota(jnp.int32, (count, columns), 0)
    lane = lax.broadcasted_iota(jnp.int32, (count, columns), 1)
    chosen = (line == lane + lax.axis_index("space") * columns).astype(BF16)
    mine = pl.ds(pl.multiple_of(lax.axis_index("tile") * rows, rows), rows)
    for p in range(2 * half):
        for part in range(2):
            value = held[p, part, mine, :]
            high = value.astype(BF16)
            middle, low = split(value - high.astype(F32))
            part_out[p, part] = (
                jnp.dot(high, chosen, preferred_element_type=F32)
                + jnp.dot(middle, chosen, preferred_element_type=F32)
            ) + jnp.dot(low, chosen, preferred_element_type=F32)
    depth = min(total, 256)
    for n in range(total // depth):
        while copies and sum(depths[: len(depths) - len(copies)]) < (n + 1) * depth:
            copies.pop(0).wait()
        here = pl.ds(n * depth, depth)

        def mix(a, carry):
            given = jnp.concatenate([tau[0, a, here, :], tau[1, a, here, :]], axis=1)
            mixed = product(split(given), weights)
            for g in range(2):
                left[g, a, here, :] = mixed[:, 4 * g * rows : (4 * g + 2) * rows]
                right[g, a, here, :] = mixed[:, (4 * g + 2) * rows : (4 * g + 4) * rows]
            return carry

        for a in range(spin):
            mix(a, 0)
    last.wait()
    width = rows * spin
    for g, out in enumerate(outs):
        left_hi, left_lo = split(jnp.concatenate([left[g, a] for a in range(spin)], axis=1))
        right_hi, right_lo = split(jnp.concatenate([right[g, a] for a in range(spin)], axis=1))
        pair = (dot_tn(left_hi, right_hi) + dot_tn(left_hi, right_lo) + dot_tn(left_lo, right_hi)) * scale
        top = jnp.concatenate([pair[2 * a * rows : (2 * a + 1) * rows] for a in range(spin)], axis=0)
        low = jnp.concatenate([pair[(2 * a + 1) * rows : (2 * a + 2) * rows] for a in range(spin)], axis=0)
        lane = lax.broadcasted_iota(jnp.int32, top.shape, 1)
        swapped = jnp.concatenate(
            [pltpu.roll(low[:, 2 * a * rows : 2 * (a + 1) * rows], rows, 1) for a in range(spin)], axis=1
        )
        pair = top + jnp.where(lane % (2 * rows) < rows, -swapped, swapped)
        pair_hi, pair_lo = split(pair)
        placed = jnp.dot(pair_hi, placing[...], preferred_element_type=F32) + jnp.dot(
            pair_lo, placing[...], preferred_element_type=F32
        )
        for a in range(spin):
            for n in range(2):
                value = placed[a * rows : (a + 1) * rows, n * width : (n + 1) * width]
                for c in range(width // LANES):
                    woven[n, c, pl.ds(a, rows, stride=spin), :] = value[:, c * LANES : (c + 1) * LANES]
        for n in range(2):
            for c in range(width // LANES):
                out[n, :, c * LANES : (c + 1) * LANES] = woven[n, c]


def lane_order(rows, spin):
    size = 2 * rows * spin
    lane = lax.iota(jnp.int32, size)
    a, part, i = lane // (2 * rows), lane // rows % 2, lane % rows
    target = part * rows * spin + i * spin + a
    return (target[:, None] == lane[None, :]).astype(BF16)


def pair_contraction(blocks, order, own, other, pieces, scale):
    half, _, count, _ = own.shape
    spin = pieces[0][0].shape[1]
    depths = [depth for _, depth in pieces]
    total = sum(depths)
    rows = count // lax.axis_size("tile")
    mixed = pltpu.VMEM((2, spin, total, 2 * rows), F32)
    return pl.pallas_call(
        functools.partial(pair_kernel, depths=depths, scale=scale),
        in_specs=[pl.BlockSpec(memory_space=pltpu.SMEM)]
        + [pl.BlockSpec(memory_space=pltpu.HBM)] * (3 + len(pieces)),
        out_specs=[pl.BlockSpec(memory_space=pltpu.VMEM)] * 3,
        out_shape=[jax.ShapeDtypeStruct((2, rows * spin, rows * spin), F32)] * 2
        + [jax.ShapeDtypeStruct((2 * half, 2, rows, count // lax.axis_size("space")), F32)],
        scratch_shapes=[
            mixed,
            mixed,
            pltpu.VMEM((2, rows * spin // LANES, rows * spin, LANES), F32),
            pltpu.VMEM((2, spin, total, count), F32),
            pltpu.VMEM((2 * half, 2, count, count), F32),
            pltpu.VMEM(order.shape, BF16),
            pltpu.SemaphoreType.DMA((len(pieces) + 3,)),
        ],
        compiler_params=pltpu.CompilerParams(vmem_limit_bytes=PAIR_VMEM),
        name="pair_contraction",
    )(blocks, own, other, order, *[piece for piece, _ in pieces])


def per_device(eigenvectors, perambulator, momenta, graph_blocks):
    space_count = lax.axis_size("space")
    tile_count = lax.axis_size("tile")
    space_index = lax.axis_index("space")
    tile_index = lax.axis_index("tile")
    device = space_index * tile_count + tile_index
    _, count, colours, sites = eigenvectors.shape
    order = perambulator.shape[2]
    norm = 1.0 / math.sqrt(colours * sites * space_count * tile_count)
    planes = eigenvectors.transpose(0, 2, 1, 3)

    def gram(started):
        return local_gram(planes, momenta, norm, started)

    spin = order // count
    blocks = jnp.stack([graph_blocks[device ^ 1], graph_blocks[device]])
    extra = [blocks, lane_order(count // tile_count, spin)]
    own, other, pieces, extra = exchange_everything(perambulator, gram, extra)
    half = momenta.shape[0] // 2
    own = own.reshape(half, 2, count, count)
    other = other.reshape(half, 2, count, count)
    scale = 1.0 / (count * math.sqrt(order))
    away, kept, elementals = pair_contraction(*extra, own, other, pieces, scale)
    return elementals, (kept + swap(away, "tile", 0))[None]


def solution(mesh):
    in_specs = (P(None, None, None, ("space", "tile")), P(None, "space", None), P(), P())
    out_specs = (P(None, None, "tile", "space"), P(("space", "tile"), None, None, None))
    return jax.shard_map(
        per_device, mesh=mesh, in_specs=in_specs, out_specs=out_specs, check_vma=False
    )
```

```python
import functools
import math

import jax
import jax.numpy as jnp
from jax import lax
from jax.experimental import pallas as pl
from jax.experimental.pallas import tpu as pltpu
from jax.sharding import PartitionSpec as P

LATTICE_EDGE = 64
LANES = 128
F32 = jnp.float32
BF16 = jnp.bfloat16
WAVE_ENDS = (-2, 0)
PASS_ENDS = (-1, 1, 2)
GRAM_VMEM = 53 * 1024 * 1024
PAIR_VMEM = 48 * 1024 * 1024


def bits_of(count):
    return range(count.bit_length() - 1)


def split(value):
    high = value.astype(BF16)
    return high, (value - high.astype(F32)).astype(BF16)


def dot_nt(left, right):
    return lax.dot_general(left, right, (((1,), (1,)), ((), ())), preferred_element_type=F32)


def product(left, right):
    return dot_nt(left[0], right[0]) + dot_nt(left[0], right[1]) + dot_nt(left[1], right[0])


def dot_tn(left, right):
    return lax.dot_general(left, right, (((0,), (0,)), ((), ())), preferred_element_type=F32)


def gram_kernel(momenta, vectors, *refs, width, norm):
    away, kept, held, arrived = refs[-4:]
    _, colours, _, sites = vectors.shape
    core = lax.rem(lax.axis_index("tile"), 2)
    first_site = (lax.axis_index("space") * lax.axis_size("tile") + lax.axis_index("tile")) * sites
    chunks = sites // width
    copies = []
    for colour in range(colours):
        for chunk in range(chunks):
            lanes = pl.ds(chunk * width, width)
            copies.append(
                pltpu.make_async_copy(
                    vectors.at[:, colour, :, lanes], held.at[:, colour, :, lanes], arrived.at[len(copies)]
                )
            )
    for copy in copies:
        copy.start()
    half = kept.shape[0]
    sums = []
    for total, first in ((kept, core * half), (away, (1 - core) * half)):
        for p in range(half):
            phases = []
            for chunk in range(chunks):
                site = first_site + chunk * width + lax.broadcasted_iota(jnp.int32, (1, width), 1)
                wave = (
                    momenta[first + p, 0] * (site % LATTICE_EDGE)
                    + momenta[first + p, 1] * (site // LATTICE_EDGE % LATTICE_EDGE)
                    + momenta[first + p, 2] * (site // (LATTICE_EDGE * LATTICE_EDGE))
                ) % LATTICE_EDGE
                theta = wave.astype(F32) * (2.0 * math.pi / LATTICE_EDGE)
                phases.append((jnp.cos(theta), jnp.sin(theta)))
            sums.append((total, p, phases))
    held_sums = {}
    for n, copy in enumerate(copies):
        copy.wait()
        chunk = n % chunks
        real = held[0, n // chunks, :, chunk * width : (chunk + 1) * width]
        imag = held[1, n // chunks, :, chunk * width : (chunk + 1) * width]
        left = split(real), split(imag), split(real - imag)
        for number, (_, _, phases) in enumerate(sums):
            cosine, sine = phases[chunk]
            phased_real = cosine * real + sine * imag
            phased_imag = cosine * imag - sine * real
            by_real = product(left[2], split(phased_real))
            from_real = product(left[0], split(phased_imag - phased_real))
            from_imag = product(left[1], split(phased_real + phased_imag))
            parts = by_real, from_real, from_imag
            held_sums[number] = parts if n == 0 else [old + new for old, new in zip(held_sums[number], parts)]
    for number, (total, p, _) in enumerate(sums):
        by_real, from_real, from_imag = held_sums[number]
        total[p, 0] = (by_real + from_imag) * norm
        total[p, 1] = (by_real + from_real) * norm


def local_gram(planes, momenta, norm, started):
    _, colours, count, sites = planes.shape
    half = momenta.shape[0] // 2
    width = min(sites, 512)
    return pl.pallas_call(
        functools.partial(gram_kernel, width=width, norm=norm),
        in_specs=[pl.BlockSpec(memory_space=pltpu.SMEM), pl.BlockSpec(memory_space=pltpu.HBM)]
        + [pl.BlockSpec(memory_space=pl.ANY)] * len(started),
        out_specs=[pl.BlockSpec(memory_space=pltpu.VMEM)] * 2,
        out_shape=[jax.ShapeDtypeStruct((half, 2, count, count), F32)] * 2,
        scratch_shapes=[
            pltpu.VMEM(planes.shape, F32),
            pltpu.SemaphoreType.DMA((colours * sites // width,)),
        ],
        compiler_params=pltpu.CompilerParams(vmem_limit_bytes=GRAM_VMEM),
        cost_estimate=pl.CostEstimate(
            flops=48 * half * count * count * colours * sites,
            bytes_accessed=8 * count * colours * sites,
            transcendentals=0,
        ),
        name="local_gram",
    )(momenta, planes, *started)


def together(*values):
    anywhere = pl.BlockSpec(memory_space=pl.ANY)
    return pl.pallas_call(
        lambda *refs: None,
        in_specs=[anywhere] * len(values),
        out_specs=[anywhere] * len(values),
        out_shape=[jax.ShapeDtypeStruct(value.shape, value.dtype) for value in values],
        input_output_aliases={n: n for n in range(len(values))},
        compiler_params=pltpu.CompilerParams(vmem_limit_bytes=1024 * 1024),
        name="together",
    )(*values)


def swap(value, axis, bit):
    size = lax.axis_size(axis)
    return lax.ppermute(value, axis, [(i, i ^ (1 << bit)) for i in range(size)])


def shift(value, axis, by):
    size = lax.axis_size(axis)
    return lax.ppermute(value, axis, [(i, i + by) for i in range(size) if 0 <= i + by < size])


def own_bit(axis, bit):
    return (lax.axis_index(axis) >> bit) & 1


def halve(value, axis, bit):
    mine = own_bit(axis, bit)
    half = value.shape[0] // 2
    away = lax.dynamic_slice_in_dim(value, (1 - mine) * half, half, 0)
    kept = lax.dynamic_slice_in_dim(value, mine * half, half, 0)
    return kept + swap(away, axis, bit)


def both(value, axis, bit):
    return value + swap(value, axis, bit)


def double(value, axis, bit):
    other = swap(value, axis, bit)
    return jnp.where(
        own_bit(axis, bit) == 0,
        jnp.concatenate([value, other]),
        jnp.concatenate([other, value]),
    )


def deal_kernel(tau, travel, whole, fetched, arrived, *, by_core, by_tile, tiles):
    parts, spin, _, count = travel.shape
    tile = lax.axis_index("tile")
    core = lax.rem(tile, 2)
    groups = [(pl.multiple_of(core * by_core, 8), by_core, whole, 0)]
    shared = 2 * by_core
    if by_tile:
        for n in range(tiles // 2):
            first = pl.multiple_of(shared + (2 * n + core) * by_tile, 8)
            groups.append((first, by_tile, whole, by_core + n * by_tile))
    copies, top = [], 0
    for part in range(parts):
        for first, depth, *_ in groups:
            copies.append(
                pltpu.make_async_copy(
                    tau.at[part, pl.ds(first, depth)], fetched.at[pl.ds(top, depth)], arrived.at[len(copies)]
                )
            )
            top += depth
    for copy in copies:
        copy.start()
    for copy in copies:
        copy.wait()
    rows = fetched[...]
    width = min(count, LANES)
    line = lax.broadcasted_iota(jnp.int32, (spin * width, spin * width), 0)
    lane = lax.broadcasted_iota(jnp.int32, (spin * width, spin * width), 1)
    order = (line == lane % width * spin + lane // width).astype(BF16)
    blocks = count // width
    value = jnp.concatenate(
        [rows[:, block * spin * width : (block + 1) * spin * width] for block in range(blocks)], axis=0
    )
    high = value.astype(BF16)
    middle, low = split(value - high.astype(F32))
    moved = jnp.dot(jnp.concatenate([high, middle, low], axis=0), order, preferred_element_type=F32)
    size = value.shape[0]
    moved = moved[:size] + moved[size : 2 * size] + moved[2 * size :]
    top = 0
    for block in range(blocks):
        for part in range(parts):
            for _, depth, target, at in groups:
                for a in range(spin):
                    target[part, a, at : at + depth, block * width : (block + 1) * width] = moved[
                        top : top + depth, a * width : (a + 1) * width
                    ]
                top += depth
    for part in range(parts):
        for a in range(spin):
            travel[part, a, :by_core, :] = whole[part, a, :by_core, :]
            if by_tile:
                mine = pl.ds(pl.multiple_of(by_core + tile // 2 * by_tile, 8), by_tile)
                travel[part, a, by_core : by_core + by_tile, :] = whole[part, a, mine, :]


def deal(part, spin, by_core, by_tile):
    parts, _, order = part.shape
    tiles = lax.axis_size("tile")
    shape = (parts, spin, by_core + by_tile, order // spin)
    whole = (parts, spin, by_core + tiles // 2 * by_tile, order // spin)
    return pl.pallas_call(
        functools.partial(deal_kernel, by_core=by_core, by_tile=by_tile, tiles=tiles),
        in_specs=[pl.BlockSpec(memory_space=pltpu.HBM)],
        out_specs=[pl.BlockSpec(memory_space=pltpu.VMEM)] * 2,
        out_shape=[jax.ShapeDtypeStruct(shape, F32), jax.ShapeDtypeStruct(whole, F32)],
        scratch_shapes=[
            pltpu.VMEM((parts * (by_core + tiles // 2 * by_tile), order), F32),
            pltpu.SemaphoreType.DMA((parts * (1 + tiles // 2),)),
        ],
        compiler_params=pltpu.CompilerParams(vmem_limit_bytes=PAIR_VMEM),
        name="deal",
    )(part)


def exchange_everything(part, gram, extra):
    space_bits, tile_bits = bits_of(lax.axis_size("space")), bits_of(lax.axis_size("tile"))
    tile_count = lax.axis_size("tile")
    sources = part.shape[1]
    shared = sources // 4
    if (sources - shared) // tile_count % 8:
        shared = sources
    by_core, by_tile = shared // 2, (sources - shared) // tile_count
    mixed, whole = deal(part, 4, by_core, by_tile)
    pieces = [(whole, whole.shape[2])]

    slots = {0: mixed}
    places = lax.axis_size("space")

    def wave_of(mask):
        return 2 if mask == 3 else mask.bit_count() - 1

    waves = max(wave_of(mask) for mask in range(1, places)) + 1
    masks_of = [[mask for mask in range(1, places) if wave_of(mask) == w] for w in range(waves)]

    def wave(w):
        bits = [1 if mask == 3 else (mask & -mask).bit_length() - 1 for mask in masks_of[w]]
        given = [whole if mask == 1 else slots[mask ^ (1 << bit)] for mask, bit in zip(masks_of[w], bits)]
        return [swap(value, "space", bit) for value, bit in zip(given, bits)]

    def passing(w):
        arrived = []
        if by_tile:
            held = jnp.concatenate([slots[mask][:, :, by_core:] for mask in masks_of[w] if mask > 1], axis=2)
            for bit in tile_bits[1:]:
                arrived.append(swap(held, "tile", bit))
                held = jnp.concatenate([held, arrived[-1]], axis=2)
        return arrived

    coming = {}

    def land(rows, step):
        landing = [w for w in range(waves) if wave_end(w) == step]
        values = [coming.pop(("wave", w)) for w in landing]
        passed = [coming.pop(("pass", w)) for w in range(waves) if pass_end(w) == step]
        flat = [piece for group in values + passed for piece in group]
        if flat:
            rows, *flat = together(rows, *flat)
            pieces.extend((piece, piece.shape[2]) for piece in flat)
            for w in landing:
                slots.update(zip(masks_of[w], flat))
                flat = flat[len(masks_of[w]) :]
            if 0 in landing and by_tile:
                first = by_core + lax.axis_index("tile") // 2 * by_tile
                mine = lax.dynamic_slice_in_dim(slots[1], first, by_tile, 2)
                slots[1] = jnp.concatenate([slots[1][:, :, :by_core], mine], axis=2)
        for w in landing:
            if w + 1 < waves:
                coming["wave", w + 1] = wave(w + 1)
            coming["pass", w] = passing(w)
        return rows

    steps = [(halve, "tile", b) for b in tile_bits[1:]]
    steps += [(halve, "space", b) for b in space_bits[:1]]
    steps += [(both, "space", b) for b in space_bits[:0:-1]]
    middle = len(steps) - 2
    steps += [(double, axis, b) for step, axis, b in steps[::-1] if step is halve]

    def wave_end(w):
        return -1 if w == 0 else middle + WAVE_ENDS[w - 1] if w <= len(WAVE_ENDS) else len(steps) + w

    def pass_end(w):
        return middle + PASS_ENDS[w] if w < len(PASS_ENDS) else len(steps) + waves + w

    coming["wave", 0] = wave(0)
    away, kept = gram([mixed])
    away = land(away.reshape(-1, kept.shape[-1]), -1)
    rows = kept.reshape(-1, kept.shape[-1]) + swap(away, "tile", 0)
    for n, (step, axis, bit) in enumerate(steps):
        rows = step(rows, axis, bit)
        if n == middle - 1:
            rows, *extra = together(rows, *extra)
        rows = land(rows, n)
    for n in range(len(steps), len(steps) + 2 * waves):
        rows = land(rows, n)
    return rows, swap(rows, "tile", 0), pieces, extra


def pair_kernel(blocks, own, other, order, *refs, depths, scale):
    sources = refs[: len(depths)]
    away, kept, part_out, left, right, woven, tau, held, placing, arrived = refs[len(depths) :]
    _, spin, total, count = tau.shape
    outs = (away, kept)
    rows = left.shape[3] // 2
    tiles = count // rows
    half = own.shape[0]
    core = lax.rem(lax.axis_index("tile"), 2)
    gathered = [
        pltpu.make_async_copy(own, held.at[pl.ds(core * half, half)], arrived.at[len(depths)]),
        pltpu.make_async_copy(other, held.at[pl.ds((1 - core) * half, half)], arrived.at[len(depths) + 1]),
    ]
    copies, first = [], 0
    for n, depth in enumerate(depths):
        target = tau.at[:, :, pl.ds(first, depth)]
        copies.append(pltpu.make_async_copy(sources[n].at[:, :, pl.ds(0, depth)], target, arrived.at[n]))
        first += depth
    last = pltpu.make_async_copy(order, placing, arrived.at[len(depths) + 2])
    for copy in [*gathered, *copies, last]:
        copy.start()
    for copy in gathered:
        copy.wait()
    real_rows, imag_rows = [], []
    for side in range(4):
        block = blocks[side // 2, side % 2]
        p = block // tiles
        start = pl.multiple_of(block % tiles * rows, rows)
        real = held[p, 0, pl.ds(start, rows), :]
        imag = held[p, 1, pl.ds(start, rows), :]
        real_rows += [real, imag]
        imag_rows += [-imag, real]
    weights = split(
        jnp.concatenate([jnp.concatenate(real_rows, axis=0), jnp.concatenate(imag_rows, axis=0)], axis=1)
    )
    columns = part_out.shape[3]
    line = lax.broadcasted_iota(jnp.int32, (count, columns), 0)
    lane = lax.broadcasted_iota(jnp.int32, (count, columns), 1)
    chosen = (line == lane + lax.axis_index("space") * columns).astype(BF16)
    mine = pl.ds(pl.multiple_of(lax.axis_index("tile") * rows, rows), rows)
    for p in range(2 * half):
        for part in range(2):
            value = held[p, part, mine, :]
            high = value.astype(BF16)
            middle, low = split(value - high.astype(F32))
            part_out[p, part] = (
                jnp.dot(high, chosen, preferred_element_type=F32)
                + jnp.dot(middle, chosen, preferred_element_type=F32)
            ) + jnp.dot(low, chosen, preferred_element_type=F32)
    depth = min(total, 256)
    for n in range(total // depth):
        while copies and sum(depths[: len(depths) - len(copies)]) < (n + 1) * depth:
            copies.pop(0).wait()
        here = pl.ds(n * depth, depth)

        def mix(a, carry):
            given = jnp.concatenate([tau[0, a, here, :], tau[1, a, here, :]], axis=1)
            mixed = product(split(given), weights)
            for g in range(2):
                left[g, a, here, :] = mixed[:, 4 * g * rows : (4 * g + 2) * rows]
                right[g, a, here, :] = mixed[:, (4 * g + 2) * rows : (4 * g + 4) * rows]
            return carry

        for a in range(spin):
            mix(a, 0)
    last.wait()
    width = rows * spin
    for g, out in enumerate(outs):
        left_hi, left_lo = split(jnp.concatenate([left[g, a] for a in range(spin)], axis=1))
        right_hi, right_lo = split(jnp.concatenate([right[g, a] for a in range(spin)], axis=1))
        pair = (dot_tn(left_hi, right_hi) + dot_tn(left_hi, right_lo) + dot_tn(left_lo, right_hi)) * scale
        top = jnp.concatenate([pair[2 * a * rows : (2 * a + 1) * rows] for a in range(spin)], axis=0)
        low = jnp.concatenate([pair[(2 * a + 1) * rows : (2 * a + 2) * rows] for a in range(spin)], axis=0)
        lane = lax.broadcasted_iota(jnp.int32, top.shape, 1)
        swapped = jnp.concatenate(
            [pltpu.roll(low[:, 2 * a * rows : 2 * (a + 1) * rows], rows, 1) for a in range(spin)], axis=1
        )
        pair = top + jnp.where(lane % (2 * rows) < rows, -swapped, swapped)
        pair_hi, pair_lo = split(pair)
        placed = jnp.dot(pair_hi, placing[...], preferred_element_type=F32) + jnp.dot(
            pair_lo, placing[...], preferred_element_type=F32
        )
        for a in range(spin):
            for n in range(2):
                value = placed[a * rows : (a + 1) * rows, n * width : (n + 1) * width]
                for c in range(width // LANES):
                    woven[n, c, pl.ds(a, rows, stride=spin), :] = value[:, c * LANES : (c + 1) * LANES]
        for n in range(2):
            for c in range(width // LANES):
                out[n, :, c * LANES : (c + 1) * LANES] = woven[n, c]


def lane_order(rows, spin):
    size = 2 * rows * spin
    lane = lax.iota(jnp.int32, size)
    a, part, i = lane // (2 * rows), lane // rows % 2, lane % rows
    target = part * rows * spin + i * spin + a
    return (target[:, None] == lane[None, :]).astype(BF16)


def pair_contraction(blocks, order, own, other, pieces, scale):
    half, _, count, _ = own.shape
    spin = pieces[0][0].shape[1]
    depths = [depth for _, depth in pieces]
    total = sum(depths)
    rows = count // lax.axis_size("tile")
    mixed = pltpu.VMEM((2, spin, total, 2 * rows), F32)
    return pl.pallas_call(
        functools.partial(pair_kernel, depths=depths, scale=scale),
        in_specs=[pl.BlockSpec(memory_space=pltpu.SMEM)]
        + [pl.BlockSpec(memory_space=pltpu.HBM)] * (3 + len(pieces)),
        out_specs=[pl.BlockSpec(memory_space=pltpu.VMEM)] * 3,
        out_shape=[jax.ShapeDtypeStruct((2, rows * spin, rows * spin), F32)] * 2
        + [jax.ShapeDtypeStruct((2 * half, 2, rows, count // lax.axis_size("space")), F32)],
        scratch_shapes=[
            mixed,
            mixed,
            pltpu.VMEM((2, rows * spin // LANES, rows * spin, LANES), F32),
            pltpu.VMEM((2, spin, total, count), F32),
            pltpu.VMEM((2 * half, 2, count, count), F32),
            pltpu.VMEM(order.shape, BF16),
            pltpu.SemaphoreType.DMA((len(pieces) + 3,)),
        ],
        compiler_params=pltpu.CompilerParams(vmem_limit_bytes=PAIR_VMEM),
        name="pair_contraction",
    )(blocks, own, other, order, *[piece for piece, _ in pieces])


def per_device(eigenvectors, perambulator, momenta, graph_blocks):
    space_count = lax.axis_size("space")
    tile_count = lax.axis_size("tile")
    space_index = lax.axis_index("space")
    tile_index = lax.axis_index("tile")
    device = space_index * tile_count + tile_index
    _, count, colours, sites = eigenvectors.shape
    order = perambulator.shape[2]
    norm = 1.0 / math.sqrt(colours * sites * space_count * tile_count)
    planes = eigenvectors.transpose(0, 2, 1, 3)

    def gram(started):
        return local_gram(planes, momenta, norm, started)

    spin = order // count
    blocks = jnp.stack([graph_blocks[device ^ 1], graph_blocks[device]])
    extra = [blocks, lane_order(count // tile_count, spin)]
    own, other, pieces, extra = exchange_everything(perambulator, gram, extra)
    half = momenta.shape[0] // 2
    own = own.reshape(half, 2, count, count)
    other = other.reshape(half, 2, count, count)
    scale = 1.0 / (count * math.sqrt(order))
    away, kept, elementals = pair_contraction(*extra, own, other, pieces, scale)
    return elementals, (kept + swap(away, "tile", 0))[None]


def solution(mesh):
    in_specs = (P(None, None, None, ("space", "tile")), P(None, "space", None), P(), P())
    out_specs = (P(None, None, "tile", "space"), P(("space", "tile"), None, None, None))
    return jax.shard_map(
        per_device, mesh=mesh, in_specs=in_specs, out_specs=out_specs, check_vma=False
    )
```
